512 devices in a mesh: pipe: 4 (over x), tm: 32 (over y_lo, z), dp: 4 (over y_hi, core).
Axes of the slice: x: 4, y: 8 (y_hi: 2, y_lo: 4; y = y_hi * 4 + y_lo), z: 8, core: 2. Of those that a mesh axis runs over, the one named last changes fastest.
Arguments:
- video: bfloat16 [4, 4, 64, 64, 320], P(None, 'dp', 'tm'), may hold values from -6 to 6
- cotangent: bfloat16 [4, 4, 64, 64, 320], P(None, 'dp', 'tm'), may hold values from -6 to 6
- timesteps: int32 [4, 4], P(None, 'dp'), may hold values from 0 to 999
- conv_weight: bfloat16 [4, 3, 320, 320], P('pipe'), may hold values from -0.1875 to 0.1875
- out_weight: bfloat16 [4, 320, 320], P('pipe'), may hold values from -0.3125 to 0.3125
Outputs:
- conv_grad: float32 [4, 3, 320, 320], P('pipe')
- out_grad: float32 [4, 320, 320], P('pipe')
The draws below stay inside these ranges and needn't reach their ends.
All inputs are finite; a program needn't handle non-finite values.
Results may differ from the reference program's by a relative error of at most 0.012.
Values may be sent and summed in bfloat16 or wider, within the bound.
A program may use at most 64 MiB of HBM per device.

```python
import math
import jax
import jax.numpy as jnp
from jax import lax

C = 320
PIX = 64
MICRO = 4
TSTEPS = 1000
SECTIONS = 4
B = 4
FRAMES = 64


def touch_ends(array, rng, smallest, largest):
    longest = array.shape.index(max(array.shape))
    spots = []
    for shift in (0, 1):
        where = [jax.random.randint(jax.random.fold_in(rng, axis), (), 0, length) for axis, length in enumerate(array.shape)]
        where[longest] = (where[longest] + shift) % array.shape[longest]
        spots.append(tuple(where))
    return array.at[spots[0]].set(smallest).at[spots[1]].set(largest)


def level_of(key, extent, cuts, low, top_value):
    level, own = 1.0, jax.random.fold_in(key, 6)
    for axis_at, parts in cuts:
        steps = jnp.exp(jax.random.uniform(jax.random.fold_in(own, axis_at), (parts,), jnp.float32, low / len(cuts), top_value / len(cuts)))
        level = level * jnp.repeat(steps, extent[axis_at] // parts).reshape([-1 if axis == axis_at else 1 for axis in range(len(extent))])
    return level


def bell_draw(own_key, extent, scale, most, cuts=(), kind=jnp.bfloat16):
    values = scale * jax.random.normal(own_key, extent, jnp.float32)
    if cuts:
        values = values * level_of(own_key, extent, cuts, -0.22, 0.18)
    return jnp.clip(values, -most, most).astype(kind)


def setup_inputs(seed: int = 0) -> dict:
    seeds = jax.random.split(jax.random.key(seed), 6)
    video = bell_draw(seeds[0], (MICRO, B, FRAMES, PIX, C), 1.0, 6.0, ((1, 4), (2, 32)))
    cotangent = bell_draw(seeds[1], (MICRO, B, FRAMES, PIX, C), 1.0, 6.0, ((1, 4), (2, 32)))
    timesteps = touch_ends(jax.random.randint(seeds[2], (MICRO, B), 0, TSTEPS), jax.random.fold_in(seeds[2], 1), 0, TSTEPS - 1).astype(jnp.int32)
    conv_weight = bell_draw(seeds[3], (SECTIONS, 3, C, C), (3 * C) ** -0.5, 0.1875, ((0, 4),))
    out_weight = bell_draw(seeds[4], (SECTIONS, C, C), C ** -0.5, 0.3125, ((0, 4),))
    return dict(video=video, cotangent=cotangent, timesteps=timesteps, conv_weight=conv_weight, out_weight=out_weight)


EPSILON = 1e-06

def embed(times):
    half = C // 2
    index = jnp.arange(half).astype(jnp.float32)
    freq = jnp.exp(index * (-math.log(10000.0) / half))
    angle = times.astype(jnp.float32)[..., None] * freq
    return jnp.concatenate([jnp.sin(angle), jnp.cos(angle)], -1)

def block_forward(inputs, conv, outw, emb_rows):
    x_float = inputs.astype(jnp.float32)
    inv_rms = lax.rsqrt(lax.optimization_barrier(jnp.mean(x_float * x_float, -1, keepdims=True)) + EPSILON)
    normed = x_float * inv_rms
    norm_low = normed.astype(jnp.bfloat16)
    padded = jnp.pad(norm_low, ((0, 0), (1, 1), (0, 0), (0, 0)))
    frames = inputs.shape[1]
    pre_act = emb_rows[:, None, None, :]
    for offset in range(3):
        pre_act = pre_act + jnp.einsum('bfpc,cd->bfpd', padded[:, offset:offset + frames].astype(jnp.float32), conv[offset].astype(jnp.float32))
    active = jax.nn.silu(pre_act).astype(jnp.bfloat16)
    result = (x_float + jnp.einsum('bfpc,cd->bfpd', active.astype(jnp.float32), outw.astype(jnp.float32))).astype(jnp.bfloat16)
    return (result, (inv_rms, normed, padded, pre_act, active))

def block_backward(grad_out, conv, outw, saved):
    inv_rms, normed, padded, pre_act, active = saved
    frames = normed.shape[1]
    grad_float = grad_out.astype(jnp.float32)
    out_term = jnp.einsum('bfpc,bfpd->cd', active.astype(jnp.float32), grad_float)
    grad_act = jnp.einsum('bfpd,cd->bfpc', grad_float, outw.astype(jnp.float32))
    sigma = jax.nn.sigmoid(pre_act)
    grad_pre = (grad_act * sigma * (1.0 + pre_act * (1.0 - sigma))).astype(jnp.bfloat16)
    grad_pad = jnp.pad(grad_pre, ((0, 0), (1, 1), (0, 0), (0, 0)))
    conv_terms = []
    grad_norm = jnp.zeros(normed.shape, jnp.float32)
    for offset in range(3):
        conv_terms.append(jnp.einsum('bfpc,bfpd->cd', padded[:, offset:offset + frames].astype(jnp.float32), grad_pre.astype(jnp.float32)))
        grad_norm = grad_norm + jnp.einsum('bfpd,cd->bfpc', grad_pad[:, 2 - offset:2 - offset + frames].astype(jnp.float32), conv[offset].astype(jnp.float32))
    incoming_gradient = grad_float + inv_rms * (grad_norm - normed * lax.optimization_barrier(jnp.mean(grad_norm * normed, -1, keepdims=True)))
    return (incoming_gradient.astype(jnp.bfloat16), jnp.stack(conv_terms), out_term)

def reference(video, cotangent, timesteps, conv_weight, out_weight):
    embedded = embed(timesteps)
    conv_total = jnp.zeros((SECTIONS, 3, C, C), jnp.float32)
    out_total = jnp.zeros((SECTIONS, C, C), jnp.float32)
    for micro_index in range(MICRO):
        hidden = video[micro_index]
        saved_all = []
        for section in range(SECTIONS):
            hidden, saved = block_forward(hidden, conv_weight[section], out_weight[section], embedded[micro_index])
            saved_all.append(saved)
        grad_now = cotangent[micro_index]
        for section in range(SECTIONS - 1, -1, -1):
            grad_now, conv_term, out_term = block_backward(grad_now, conv_weight[section], out_weight[section], saved_all[section])
            conv_total = conv_total.at[section].add(conv_term)
            out_total = out_total.at[section].add(out_term)
    scale = 1.0 / math.sqrt(MICRO * B * FRAMES * PIX)
    return (conv_total * scale, out_total * scale)
```

```python
import functools
import math

import jax
import jax.numpy as jnp
from jax import lax
from jax.experimental import pallas as pl
from jax.experimental.pallas import tpu as pltpu
from jax.sharding import PartitionSpec as P

EPSILON = 1e-06
MESH = pl.DeviceIdType.MESH
SECTIONS = 4
C = 320
ROWS = 128
YL, Z, Y = 4, 8, 8
PA, PB = 112, 96
HA, HB = 8 * PA, 8 * PB
TOTAL = 2 * (HA + HB)
BF = jnp.bfloat16
F32 = jnp.float32


def place():
    p, t, d = lax.axis_index("pipe"), lax.axis_index("tm"), lax.axis_index("dp")
    return p, lax.div(d, 2) * YL + lax.div(t, Z), lax.rem(t, Z), lax.rem(d, 2)


def device(p, y, z, c):
    return (p, lax.rem(y, YL) * Z + z, lax.div(y, YL) * 2 + c)


def remote(src, dst, send, recv, to):
    return pltpu.make_async_remote_copy(
        src_ref=src, dst_ref=dst, send_sem=send, recv_sem=recv, device_id=to, device_id_type=MESH
    )


def each(count, fn):
    def step(i, _):
        fn(i)
        return 0

    lax.fori_loop(1, count, step, 0)


def dot(a, b):
    return jnp.dot(a, b, preferred_element_type=F32)


def dot_t(a, b):
    return lax.dot_general(a, b, (((1,), (1,)), ((), ())), preferred_element_type=F32)


def t_dot(a, b):
    return lax.dot_general(a, b, (((0,), (0,)), ((), ())), preferred_element_type=F32)


def normalize(h):
    x = h.astype(F32)
    inv = lax.rsqrt(jnp.mean(x * x, -1, keepdims=True) + EPSILON)
    return x, inv, x * inv


def before(v):
    row = lax.rem(lax.broadcasted_iota(jnp.int32, v.shape, 0), ROWS)
    return jnp.where(row < 2, 0.0, pltpu.roll(v, 2, 0))


def after(v):
    row = lax.rem(lax.broadcasted_iota(jnp.int32, v.shape, 0), ROWS)
    return jnp.where(row >= ROWS - 2, 0.0, pltpu.roll(v, v.shape[0] - 2, 0))


def reorder(source_of, v):
    r = lax.broadcasted_iota(jnp.int32, (ROWS, ROWS), 0)
    k = lax.broadcasted_iota(jnp.int32, (ROWS, ROWS), 1)
    pick = jnp.where(source_of(r) == k, 1.0, 0.0).astype(BF)
    return dot(pick, v).astype(BF)


def to_z(r):
    return lax.rem(lax.div(r, 8), 2) * 64 + lax.div(r, 16) * 8 + lax.rem(r, 8)


def to_y(r):
    return lax.div(lax.rem(r, 32), 2) * 8 + lax.div(r, 32) * 2 + lax.rem(r, 2)


def chain_kernel(
    video, cotangent, emb, convw, outw, g_ref,
    vin, cin, w, s1s, s1d, s2s, s2d, hs, ds, pre_s, hr, dr, nb, ab, d0, d1, d2,
    in_sem, z_send, z_recv, y_send, y_recv,
    x_send, x_recv, f_send, f_recv, q_send, q_recv, c_send, c_recv,
    h_send, h_recv, d_send, d_recv,
):
    p, y, z, c = place()
    yl = lax.rem(y, YL)
    ybase = y - yl
    loads = [
        pltpu.make_async_copy(video.at[p, 0], vin, in_sem.at[0]),
        pltpu.make_async_copy(cotangent.at[p, 0], cin, in_sem.at[1]),
        pltpu.make_async_copy(convw.at[0], w.at[p, pl.ds(0, 3)], in_sem.at[2]),
        pltpu.make_async_copy(outw.at[0], w.at[p, 3], in_sem.at[3]),
    ]
    for load in loads:
        load.start()

    barrier = pltpu.get_barrier_semaphore()

    def greet(to):
        pl.semaphore_signal(barrier, inc=1, device_id=to, device_id_type=MESH)

    each(SECTIONS, lambda i: greet(device(lax.rem(p + i, SECTIONS), y, z, c)))
    each(Z, lambda i: greet(device(p, y, lax.rem(z + i, Z), c)))
    each(YL, lambda i: greet(device(p, ybase + lax.rem(yl + i, YL), z, c)))
    greet(device(p, y, z, 1 - c))
    for load in loads:
        load.wait()
    pl.semaphore_wait(barrier, SECTIONS + Z + YL - 3 + 1)

    right, left = lax.rem(p + 1, SECTIONS), lax.rem(p + 3, SECTIONS)
    far = lax.rem(p + 2, SECTIONS)
    odd = jnp.where(c == 0, lax.rem(z, 2), lax.rem(y, 2))
    mine, theirs = 2 * c + odd, 2 * c + 1 - odd
    hop = 1 - 2 * odd
    pair = device(p, y + hop * c, z + hop * (1 - c), c)
    other = device(p, y, z, 1 - c)
    to_right, to_left = device(right, y, z, c), device(left, y, z, c)
    half = [pl.ds(0, C // 2), pl.ds(C // 2, C // 2)]

    def over_x(section, part, way, target):
        ref = w.at[section, mine, half[part]]
        return remote(ref, ref, x_send.at[way, part], x_recv.at[section, part], target)

    def forward(section, part, way, target):
        ref = w.at[section, mine, half[part]]
        return remote(ref, ref, f_send.at[way], f_recv.at[part], target)

    def to_pair(section, matrix):
        ref = w.at[section, matrix]
        return remote(ref, ref, q_send.at[section], q_recv.at[section], pair)

    def to_core(section, matrix):
        ref = w.at[section, matrix]
        return remote(ref, ref, c_send.at[section, matrix], c_recv.at[section, matrix], other)

    over_x(p, 0, 0, to_right).start()
    over_x(p, 1, 1, to_left).start()
    over_x(p, 1, 0, to_right).start()
    over_x(p, 0, 1, to_left).start()

    s1s[:, 0:16, :] = reorder(to_z, vin[...].reshape(ROWS, C)).reshape(Z, 16, C)
    s1s[:, 16:32, :] = reorder(to_z, cin[...].reshape(ROWS, C)).reshape(Z, 16, C)

    def z_copy(at, slot):
        return remote(s1s.at[at], s1d.at[slot], z_send.at[at], z_recv.at[slot], device(p, y, at, c))

    each(Z, lambda i: z_copy(lax.rem(z + i, Z), z).start())
    s1d[z] = s1s[z]

    over_x(left, 0, 0, to_right).wait_recv()
    forward(left, 0, 0, to_right).start()
    over_x(right, 1, 1, to_left).wait_recv()
    forward(right, 1, 1, to_left).start()

    each(Z, lambda i: z_copy(lax.rem(z + i, Z), lax.rem(z + i, Z)).wait_recv())
    s2s[:, 0:32, :] = reorder(to_y, s1d[:, 0:16, :].reshape(ROWS, C)).reshape(YL, 32, C)
    s2s[:, 32:64, :] = reorder(to_y, s1d[:, 16:32, :].reshape(ROWS, C)).reshape(YL, 32, C)

    def y_copy(at, slot):
        return remote(s2s.at[at], s2d.at[slot], y_send.at[at], y_recv.at[slot], device(p, ybase + at, z, c))

    each(YL, lambda i: y_copy(lax.rem(yl + i, YL), yl).start())
    s2d[yl] = s2s[yl]

    over_x(left, 1, 0, to_right).wait_recv()
    to_pair(left, mine).start()
    to_core(left, mine).start()
    over_x(right, 0, 1, to_left).wait_recv()
    to_pair(right, mine).start()
    to_core(right, mine).start()

    each(YL, lambda i: y_copy(lax.rem(yl + i, YL), lax.rem(yl + i, YL)).wait_recv())
    hs[0] = s2d[:, 0:32, :].reshape(ROWS, C)
    ds[3] = s2d[:, 32:64, :].reshape(ROWS, C)

    def give(value, kept, send, recv, section):
        copy = remote(value.at[section], kept.at[p], send.at[section], recv.at[p], device(section, y, z, c))

        @pl.when(p != section)
        def _():
            copy.start()

        @pl.when(p == section)
        def _():
            kept[p] = value[section]

    give(hs, hr, h_send, h_recv, 0)
    give(ds, dr, d_send, d_recv, 3)

    forward(far, 0, 0, to_right).wait_recv()
    forward(far, 1, 1, to_left).wait_recv()
    to_pair(far, mine).start()
    to_core(far, mine).start()
    for section in (left, right, far):
        to_pair(section, theirs).wait_recv()
        to_core(section, theirs).start()
    for section in (left, right, far):
        to_core(section, 2 * (1 - c)).wait_recv()
        to_core(section, 2 * (1 - c) + 1).wait_recv()

    emb_row = emb[pl.ds(p, 1), :]
    for s in range(SECTIONS):
        x, inv, normed = normalize(hs[s])
        pre = emb_row + dot(before(normed).astype(BF), w[s, 0])
        pre = pre + dot(normed.astype(BF), w[s, 1])
        pre = pre + dot(after(normed).astype(BF), w[s, 2])
        pre_s[s] = pre
        if s + 1 < SECTIONS:
            act = (pre * jax.nn.sigmoid(pre)).astype(BF)
            hs[s + 1] = (x + dot(act, w[s, 3])).astype(BF)
            give(hs, hr, h_send, h_recv, s + 1)
    for s in (3, 2, 1):
        x, inv, normed = normalize(hs[s])
        grad = ds[s]
        pre = pre_s[s]
        sig = jax.nn.sigmoid(pre)
        dpre = dot_t(grad, w[s, 3]) * sig * (1.0 + pre * (1.0 - sig))
        dnorm = dot_t(after(dpre).astype(BF), w[s, 0])
        dnorm = dnorm + dot_t(dpre.astype(BF), w[s, 1])
        dnorm = dnorm + dot_t(before(dpre).astype(BF), w[s, 2])
        mean = jnp.mean(dnorm * normed, -1, keepdims=True)
        ds[s - 1] = (grad.astype(F32) + inv * (dnorm - normed * mean)).astype(BF)
        give(ds, dr, d_send, d_recv, s - 1)

    def take(kept, value, send, recv):
        def one(i):
            m = lax.rem(p + i, SECTIONS)
            remote(value.at[0], kept.at[m], send.at[0], recv.at[m], device(m, y, z, c)).wait_recv()

        each(SECTIONS, one)

    take(hr, hs, h_send, h_recv)

    def redo(m, _):
        x, inv, normed = normalize(hr[m])
        low = normed.astype(BF)
        pre = emb[pl.ds(m, 1), :] + dot(before(normed).astype(BF), w[p, 0])
        pre = pre + dot(low, w[p, 1])
        pre = pre + dot(after(normed).astype(BF), w[p, 2])
        pre_s[m] = pre
        nb[m] = low
        ab[m] = (pre * jax.nn.sigmoid(pre)).astype(BF)
        return 0

    lax.fori_loop(0, SECTIONS, redo, 0)
    take(dr, ds, d_send, d_recv)

    def redo_back(m, _):
        pre = pre_s[m]
        sig = jax.nn.sigmoid(pre)
        dpre = dot_t(dr[m], w[p, 3]) * sig * (1.0 + pre * (1.0 - sig))
        d0[m] = after(dpre).astype(BF)
        d1[m] = dpre.astype(BF)
        d2[m] = before(dpre).astype(BF)
        return 0

    lax.fori_loop(0, SECTIONS, redo_back, 0)
    left_hand = (nb, nb, nb, ab)
    right_hand = (d0, d1, d2, dr)
    tails = []
    for k in range(4):
        term = t_dot(
            left_hand[k][...].reshape(SECTIONS * ROWS, C), right_hand[k][...].reshape(SECTIONS * ROWS, C)
        )
        g_ref[pl.ds(2 * k * C, C), :] = term[:, 0:128]
        g_ref[pl.ds((2 * k + 1) * C, C), :] = term[:, 128:256]
        tails.append(term[:, 256:320])
    g_ref[pl.ds(8 * C, C), :] = jnp.concatenate(tails[0:2], 1)
    g_ref[pl.ds(9 * C, C), :] = jnp.concatenate(tails[2:4], 1)
    g_ref[pl.ds(10 * C, TOTAL - 10 * C), :] = jnp.zeros((TOTAL - 10 * C, 128), F32)

    for part in range(2):
        over_x(p, part, 0, to_right).wait_send()
        over_x(p, part, 1, to_left).wait_send()
    forward(left, 0, 0, to_right).wait_send()
    forward(right, 1, 1, to_left).wait_send()
    for section in (left, right, far):
        to_pair(section, mine).wait_send()
        to_core(section, mine).wait_send()
        to_core(section, theirs).wait_send()
    each(Z, lambda i: z_copy(lax.rem(z + i, Z), z).wait_send())
    each(YL, lambda i: y_copy(lax.rem(yl + i, YL), yl).wait_send())

    def left_us(i):
        s = lax.rem(p + i, SECTIONS)
        to = device(s, y, z, c)
        remote(hs.at[s], hr.at[p], h_send.at[s], h_recv.at[p], to).wait_send()
        remote(ds.at[s], dr.at[p], d_send.at[s], d_recv.at[p], to).wait_send()

    each(SECTIONS, left_us)


def sum_kernel(
    scale, g, conv_out, out_out,
    sb, rb, chip, ra, rbz, ra2, rb2, fin,
    core_sem, a1s, a1r, b1s, b1r, a2s, a2r, b2s, b2r, a3s, a3r, b3s, b3r, end_sem,
):
    p, y, z, c = place()
    other = 1 - c
    sibling = device(p, y, z, other)
    barrier = pltpu.get_barrier_semaphore()

    def greet(to):
        pl.semaphore_signal(barrier, inc=1, device_id=to, device_id_type=MESH)

    def at_y(to):
        return device(p, to, z, c)

    def at_z(to):
        return device(p, y, to, c)

    def y_of(i):
        return lax.rem(y + i, Y)

    def z_of(i):
        return lax.rem(z + i, Z)

    each(Y, lambda i: greet(at_y(y_of(i))))
    each(Z, lambda i: greet(at_z(z_of(i))))
    greet(sibling)

    def rows(start, size):
        return pl.ds(pl.multiple_of(start, 16), size)

    sb[0:HA, :] = g[rows(other * HA, HA), :].astype(BF)
    sb[HA : HA + HB, :] = g[rows(2 * HA + other * HB, HB), :].astype(BF)
    pl.semaphore_wait(barrier, Y + Z - 2 + 1)

    swap = remote(sb, rb, core_sem.at[0], core_sem.at[1], sibling)
    swap.start()
    swap.wait_recv()
    chip[0:HA, :] = (g[rows(c * HA, HA), :] + rb[0:HA, :].astype(F32)).astype(BF)
    chip[HA : HA + HB, :] = (g[rows(2 * HA + c * HB, HB), :] + rb[HA : HA + HB, :].astype(F32)).astype(BF)

    def a1(to, slot):
        return remote(chip.at[rows(to * PA, PA)], ra.at[slot], a1s.at[to], a1r.at[slot], at_y(to))

    def b1(to, slot):
        return remote(chip.at[rows(HA + to * PB, PB)], rbz.at[slot], b1s.at[to], b1r.at[slot], at_z(to))

    def first(i):
        a1(y_of(i), y).start()
        b1(z_of(i), z).start()

    each(Y, first)
    ra[y] = chip[rows(y * PA, PA), :]
    rbz[z] = chip[rows(HA + z * PB, PB), :]

    def total(ref):
        value = ref[0].astype(F32)
        for i in range(1, 8):
            value = value + ref[i].astype(F32)
        return value.astype(BF)

    each(Y, lambda i: a1(y_of(i), y_of(i)).wait_recv())
    ra2[z] = total(ra)

    def a2(to, slot):
        return remote(ra2.at[slot], ra2.at[slot], a2s.at[to], a2r.at[slot], at_z(to))

    each(Z, lambda i: a2(z_of(i), z).start())
    each(Z, lambda i: b1(z_of(i), z_of(i)).wait_recv())
    rb2[y] = total(rbz)

    def b2(to, slot):
        return remote(rb2.at[slot], rb2.at[slot], b2s.at[to], b2r.at[slot], at_y(to))

    each(Y, lambda i: b2(y_of(i), y).start())

    def a3(to, slot):
        ref = fin.at[rows(c * HA + slot * PA, PA)]
        return remote(ref, ref, a3s.at[to], a3r.at[slot], at_y(to))

    def b3(to, slot):
        ref = fin.at[rows(2 * HA + c * HB + slot * PB, PB)]
        return remote(ref, ref, b3s.at[to], b3r.at[slot], at_z(to))

    each(Z, lambda i: a2(z_of(i), z_of(i)).wait_recv())
    fin[rows(c * HA + y * PA, PA), :] = total(ra2)
    each(Y, lambda i: a3(y_of(i), y).start())
    each(Y, lambda i: b2(y_of(i), y_of(i)).wait_recv())
    fin[rows(2 * HA + c * HB + z * PB, PB), :] = total(rb2)
    each(Z, lambda i: b3(z_of(i), z).start())
    each(Y, lambda i: a3(y_of(i), y_of(i)).wait_recv())

    def end_a(core):
        ref = fin.at[rows(core * HA, HA)]
        return remote(ref, ref, end_sem.at[0], end_sem.at[1], sibling)

    def end_b(core):
        ref = fin.at[rows(2 * HA + core * HB, HB)]
        return remote(ref, ref, end_sem.at[2], end_sem.at[3], sibling)

    end_a(c).start()
    each(Z, lambda i: b3(z_of(i), z_of(i)).wait_recv())
    end_b(c).start()
    end_a(other).wait_recv()
    end_b(other).wait_recv()

    for k in range(4):
        ref = conv_out.at[0, k] if k < 3 else out_out.at[0]
        ref[:, 0:128] = fin[2 * k * C : (2 * k + 1) * C, :].astype(F32) * scale
        ref[:, 128:256] = fin[(2 * k + 1) * C : (2 * k + 2) * C, :].astype(F32) * scale
        tail = fin[(8 + k // 2) * C : (9 + k // 2) * C, :].astype(F32) * scale
        ref[:, 256:320] = tail[:, 64 * (k % 2) : 64 * (k % 2) + 64]

    swap.wait_send()

    def drained(i):
        a1(y_of(i), y).wait_send()
        b1(z_of(i), z).wait_send()
        a2(z_of(i), z).wait_send()
        b2(y_of(i), y).wait_send()
        a3(y_of(i), y).wait_send()
        b3(z_of(i), z).wait_send()

    each(Y, drained)
    end_a(c).wait_send()
    end_b(c).wait_send()


def embed(times, channels):
    half = channels // 2
    index = jnp.arange(half).astype(jnp.float32)
    freq = jnp.exp(index * (-math.log(10000.0) / half))
    angle = times.astype(jnp.float32)[..., None] * freq
    return jnp.concatenate([jnp.sin(angle), jnp.cos(angle)], -1)


def body(video, cotangent, timesteps, conv_weight, out_weight):
    emb = embed(timesteps[:, 0], C)
    anywhere = pl.BlockSpec(memory_space=pl.ANY)
    vmem = pl.BlockSpec(memory_space=pltpu.VMEM)
    dma = pltpu.SemaphoreType.DMA
    stack = (SECTIONS, ROWS, C)
    partial = pl.pallas_call(
        chain_kernel,
        out_shape=jax.ShapeDtypeStruct((TOTAL, 128), F32),
        in_specs=[anywhere, anywhere, vmem, anywhere, anywhere],
        out_specs=vmem,
        scratch_shapes=[
            pltpu.VMEM((2, 64, C), BF),
            pltpu.VMEM((2, 64, C), BF),
            pltpu.VMEM((SECTIONS, 4, C, C), BF),
            pltpu.VMEM((Z, 32, C), BF),
            pltpu.VMEM((Z, 32, C), BF),
            pltpu.VMEM((YL, 64, C), BF),
            pltpu.VMEM((YL, 64, C), BF),
            pltpu.VMEM(stack, BF),
            pltpu.VMEM(stack, BF),
            pltpu.VMEM(stack, F32),
            pltpu.VMEM(stack, BF),
            pltpu.VMEM(stack, BF),
            pltpu.VMEM(stack, BF),
            pltpu.VMEM(stack, BF),
            pltpu.VMEM(stack, BF),
            pltpu.VMEM(stack, BF),
            pltpu.VMEM(stack, BF),
            dma((4,)),
            dma((Z,)), dma((Z,)), dma((YL,)), dma((YL,)),
            dma((2, 2)), dma((SECTIONS, 2)), dma((2,)), dma((2,)),
            dma((SECTIONS,)), dma((SECTIONS,)), dma((SECTIONS, 4)), dma((SECTIONS, 4)),
            dma((SECTIONS,)), dma((SECTIONS,)), dma((SECTIONS,)), dma((SECTIONS,)),
        ],
        compiler_params=pltpu.CompilerParams(
            collective_id=1, has_side_effects=True, vmem_limit_bytes=48 << 20
        ),
        name="chain",
    )(video, cotangent, emb, conv_weight, out_weight)
    rows = video.shape[0] * 4 * 64 * video.shape[3]
    return pl.pallas_call(
        functools.partial(sum_kernel, 1.0 / math.sqrt(rows)),
        out_shape=(
            jax.ShapeDtypeStruct((1, 3, C, C), F32),
            jax.ShapeDtypeStruct((1, C, C), F32),
        ),
        in_specs=[vmem],
        out_specs=(vmem, vmem),
        scratch_shapes=[
            pltpu.VMEM((HA + HB, 128), BF),
            pltpu.VMEM((HA + HB, 128), BF),
            pltpu.VMEM((HA + HB, 128), BF),
            pltpu.VMEM((8, PA, 128), BF),
            pltpu.VMEM((8, PB, 128), BF),
            pltpu.VMEM((8, PA, 128), BF),
            pltpu.VMEM((8, PB, 128), BF),
            pltpu.VMEM((TOTAL, 128), BF),
            dma((2,)),
        ]
        + [dma((8,))] * 12
        + [dma((4,))],
        compiler_params=pltpu.CompilerParams(
            collective_id=2, has_side_effects=True, vmem_limit_bytes=48 << 20
        ),
        name="sum",
    )(partial)


def solution(mesh):
    return jax.shard_map(
        body,
        mesh=mesh,
        in_specs=(
            P(None, "dp", "tm", None, None),
            P(None, "dp", "tm", None, None),
            P(None, "dp"),
            P("pipe", None, None, None),
            P("pipe", None, None),
        ),
        out_specs=(P("pipe", None, None, None), P("pipe", None, None)),
        check_vma=False,
    )
```

```python
import functools
import math

import jax
import jax.numpy as jnp
from jax import lax
from jax.experimental import pallas as pl
from jax.experimental.pallas import tpu as pltpu
from jax.sharding import PartitionSpec as P

EPSILON = 1e-06
MESH = pl.DeviceIdType.MESH
SECTIONS = 4
C = 320
ROWS = 128
YL, Z, Y = 4, 8, 8
PA, PB = 112, 96
HA, HB = 8 * PA, 8 * PB
HALF = HA + HB
CHUNK_A, CHUNK_B = ((0, 64), (64, 48)), ((0, 48), (48, 48))
QUARTER = C // 2
BF = jnp.bfloat16
F32 = jnp.float32


def place():
    p, t, d = lax.axis_index("pipe"), lax.axis_index("tm"), lax.axis_index("dp")
    return p, lax.div(d, 2) * YL + lax.div(t, Z), lax.rem(t, Z), lax.rem(d, 2)


def device(p, y, z, c):
    return (p, lax.rem(y, YL) * Z + z, lax.div(y, YL) * 2 + c)


def remote(src, dst, send, recv, to):
    return pltpu.make_async_remote_copy(
        src_ref=src, dst_ref=dst, send_sem=send, recv_sem=recv, device_id=to, device_id_type=MESH
    )


def each(count, fn):
    def step(i, _):
        fn(i)
        return 0

    lax.fori_loop(1, count, step, 0)


def dot(a, b):
    return jnp.dot(a, b, preferred_element_type=F32)


def dot_t(a, b):
    return lax.dot_general(a, b, (((1,), (1,)), ((), ())), preferred_element_type=F32)


def t_dot(a, b):
    return lax.dot_general(a, b, (((0,), (0,)), ((), ())), preferred_element_type=F32)


def normalize(h):
    x = h.astype(F32)
    inv = lax.rsqrt(jnp.mean(x * x, -1, keepdims=True) + EPSILON)
    return x, inv, x * inv


def before(v):
    row = lax.rem(lax.broadcasted_iota(jnp.int32, v.shape, 0), ROWS)
    return jnp.where(row < 2, 0.0, pltpu.roll(v, 2, 0))


def after(v):
    row = lax.rem(lax.broadcasted_iota(jnp.int32, v.shape, 0), ROWS)
    return jnp.where(row >= ROWS - 2, 0.0, pltpu.roll(v, v.shape[0] - 2, 0))


def reorder(source_of, v):
    r = lax.broadcasted_iota(jnp.int32, (ROWS, ROWS), 0)
    k = lax.broadcasted_iota(jnp.int32, (ROWS, ROWS), 1)
    pick = jnp.where(source_of(r) == k, 1.0, 0.0).astype(BF)
    return dot(pick, v).astype(BF)


def to_z(r):
    return lax.rem(lax.div(r, 8), 2) * 64 + lax.div(r, 16) * 8 + lax.rem(r, 8)


def to_y(r):
    return lax.div(lax.rem(r, 32), 2) * 8 + lax.div(r, 32) * 2 + lax.rem(r, 2)


def kernel(
    video, cotangent, times, convw, outw, fin,
    vin, cin, tin, emb, w, s1s, s1d, s2s, s2d, hs, ds, pre_s, hr, lhs, rhs,
    gown, sb, rb, chip, ra, rbz, ra2, rb2,
    in_sem, z_send, z_recv, y_send, y_recv,
    x_send, x_recv, n_send, n_recv, c_send, c_recv,
    h_send, h_recv, d_send, d_recv,
    core_sem, a1s, a1r, b1s, b1r, a2s, a2r, b2s, b2r, a3s, a3r, b3s, b3r, end_sem,
):
    p, y, z, c = place()
    yl = lax.rem(y, YL)
    ybase = y - yl
    other = 1 - c
    loads = [
        pltpu.make_async_copy(convw.at[0], w.at[p, pl.ds(0, 6)], in_sem.at[2]),
        pltpu.make_async_copy(outw.at[0], w.at[p, pl.ds(6, 2)], in_sem.at[3]),
        pltpu.make_async_copy(video.at[p, 0], vin, in_sem.at[0]),
        pltpu.make_async_copy(cotangent.at[p, 0], cin, in_sem.at[1]),
        pltpu.make_async_copy(times, tin, in_sem.at[4]),
    ]
    for load in loads:
        load.start()

    barrier = pltpu.get_barrier_semaphore()

    def greet(to):
        pl.semaphore_signal(barrier, inc=1, device_id=to, device_id_type=MESH)

    def at_x(to):
        return device(to, y, z, c)

    def at_y(to):
        return device(p, to, z, c)

    def at_z(to):
        return device(p, y, to, c)

    def x_of(i):
        return lax.rem(p + i, SECTIONS)

    def y_of(i):
        return lax.rem(y + i, Y)

    def z_of(i):
        return lax.rem(z + i, Z)

    sibling = device(p, y, z, other)
    each(SECTIONS, lambda i: greet(at_x(x_of(i))))
    each(Y, lambda i: greet(at_y(y_of(i))))
    each(Z, lambda i: greet(at_z(z_of(i))))
    greet(sibling)
    for load in loads:
        load.wait()
    pl.semaphore_wait(barrier, SECTIONS + Y + Z - 3 + 1)

    color = lax.rem((y + 2 * z) * other + (2 * y + z) * c, 4)
    step_y, step_z = other, c
    nexts = [
        device(p, lax.rem(y + step_y, Y), lax.rem(z + step_z, Z), c),
        device(p, lax.rem(y + Y - step_y, Y), lax.rem(z + Z - step_z, Z), c),
        device(p, lax.rem(y + step_z, Y), lax.rem(z + step_y, Z), c),
        device(p, lax.rem(y + Y - step_z, Y), lax.rem(z + Z - step_y, Z), c),
    ]
    parts = [pl.ds(0, QUARTER), pl.ds(0, QUARTER), pl.ds(0, QUARTER // 2), pl.ds(QUARTER // 2, QUARTER // 2)]
    quarter = [lax.rem(color + k, 4) for k in range(4)]

    def over_x(section, to):
        ref = w.at[section, 4 * c + color]
        return remote(ref, ref, x_send.at[to], x_recv.at[section], at_x(to))

    def to_next(section, way, part):
        ref = w.at[section, 4 * c + part, parts[way]]
        return remote(ref, ref, n_send.at[section, way], n_recv.at[section, way], nexts[way])

    def to_core(section, core, part):
        ref = w.at[section, 4 * core + part]
        return remote(ref, ref, c_send.at[section, part], c_recv.at[section, part], sibling)

    right, left, far = x_of(1), x_of(3), x_of(2)
    for to in (right, left, far):
        over_x(p, to).start()

    s1s[:, 0:16, :] = reorder(to_z, vin[...].reshape(ROWS, C)).reshape(Z, 16, C)
    s1s[:, 16:32, :] = reorder(to_z, cin[...].reshape(ROWS, C)).reshape(Z, 16, C)

    def z_copy(at, slot):
        return remote(s1s.at[at], s1d.at[slot], z_send.at[at], z_recv.at[slot], at_z(at))

    each(Z, lambda i: z_copy(z_of(i), z).start())
    s1d[z] = s1s[z]

    lane = lax.broadcasted_iota(jnp.int32, (1, C), 1)
    index = jnp.where(lane < C // 2, lane, lane - C // 2).astype(F32)
    freq = jnp.exp(index * (-math.log(10000.0) / (C // 2)))
    for m in range(SECTIONS):
        angle = tin[:, m : m + 1].astype(F32) * freq
        emb[m : m + 1, :] = jnp.where(lane < C // 2, jnp.sin(angle), jnp.cos(angle))

    def spread(section):
        over_x(section, p).wait_recv()
        for way in range(4):
            to_next(section, way, color).start()
        to_core(section, c, color).start()

    spread(left)
    spread(right)

    each(Z, lambda i: z_copy(z_of(i), z_of(i)).wait_recv())
    for kind in range(2):
        s2s[kind] = reorder(to_y, s1d[:, 16 * kind : 16 * kind + 16, :].reshape(ROWS, C)).reshape(YL, 32, C)

    def yl_of(i):
        return lax.rem(yl + i, YL)

    def y_copy(kind, at, slot):
        return remote(
            s2s.at[kind, at], s2d.at[kind, slot], y_send.at[kind, at], y_recv.at[kind, slot], at_y(ybase + at)
        )

    each(YL, lambda i: y_copy(0, yl_of(i), yl).start())
    spread(far)
    each(YL, lambda i: y_copy(1, yl_of(i), yl).start())
    s2d[0, yl] = s2s[0, yl]
    s2d[1, yl] = s2s[1, yl]

    def give(value, kept, send, recv, section):
        copy = remote(value.at[section], kept.at[p], send.at[section], recv.at[p], at_x(section))

        @pl.when(p != section)
        def _():
            copy.start()

        @pl.when(p == section)
        def _():
            kept[p] = value[section]

    dr = rhs.at[3]
    each(YL, lambda i: y_copy(0, yl_of(i), yl_of(i)).wait_recv())
    hs[0] = s2d[0].reshape(ROWS, C)
    give(hs, hr, h_send, h_recv, 0)

    for section in (left, right, far):
        to_next(section, 0, quarter[3]).wait_recv()
        to_core(section, c, quarter[3]).start()
        to_next(section, 1, quarter[1]).wait_recv()
        to_core(section, c, quarter[1]).start()
        to_next(section, 2, quarter[2]).wait_recv()
        to_next(section, 3, quarter[2]).wait_recv()
        to_core(section, c, quarter[2]).start()

    each(YL, lambda i: y_copy(1, yl_of(i), yl_of(i)).wait_recv())
    ds[3] = s2d[1].reshape(ROWS, C)
    give(ds, dr, d_send, d_recv, 3)

    for section in (left, right, far):
        for part in range(4):
            to_core(section, other, part).wait_recv()

    def weight(section, k):
        return w[section, 2 * k : 2 * k + 2].reshape(C, C)

    emb_row = emb[pl.ds(p, 1), :]
    for s in range(SECTIONS):
        x, inv, normed = normalize(hs[s])
        pre = emb_row + dot(before(normed).astype(BF), weight(s, 0))
        pre = pre + dot(normed.astype(BF), weight(s, 1))
        pre = pre + dot(after(normed).astype(BF), weight(s, 2))
        pre_s[s] = pre
        if s + 1 < SECTIONS:
            act = (pre * jax.nn.sigmoid(pre)).astype(BF)
            hs[s + 1] = (x + dot(act, weight(s, 3))).astype(BF)
            give(hs, hr, h_send, h_recv, s + 1)
    for s in (3, 2, 1):
        x, inv, normed = normalize(hs[s])
        grad = ds[s]
        pre = pre_s[s]
        sig = jax.nn.sigmoid(pre)
        dpre = dot_t(grad, weight(s, 3)) * sig * (1.0 + pre * (1.0 - sig))
        dnorm = dot_t(after(dpre).astype(BF), weight(s, 0))
        dnorm = dnorm + dot_t(dpre.astype(BF), weight(s, 1))
        dnorm = dnorm + dot_t(before(dpre).astype(BF), weight(s, 2))
        mean = jnp.mean(dnorm * normed, -1, keepdims=True)
        ds[s - 1] = (grad.astype(F32) + inv * (dnorm - normed * mean)).astype(BF)
        give(ds, dr, d_send, d_recv, s - 1)

    def take(kept, value, send, recv):
        def one(i):
            m = x_of(i)
            remote(value.at[0], kept.at[m], send.at[0], recv.at[m], at_x(m)).wait_recv()

        each(SECTIONS, one)

    take(hr, hs, h_send, h_recv)

    def redo(m, _):
        x, inv, normed = normalize(hr[m])
        low = normed.astype(BF)
        pre = emb[pl.ds(m, 1), :] + dot(before(normed).astype(BF), weight(p, 0))
        pre = pre + dot(low, weight(p, 1))
        pre = pre + dot(after(normed).astype(BF), weight(p, 2))
        pre_s[m] = pre
        lhs[0, m] = low
        lhs[1, m] = (pre * jax.nn.sigmoid(pre)).astype(BF)
        return 0

    lax.fori_loop(0, SECTIONS, redo, 0)
    take(dr, ds, d_send, d_recv)

    def redo_back(m, _):
        pre = pre_s[m]
        sig = jax.nn.sigmoid(pre)
        dpre = dot_t(rhs[3, m], weight(p, 3)) * sig * (1.0 + pre * (1.0 - sig))
        rhs[0, m] = after(dpre).astype(BF)
        rhs[1, m] = dpre.astype(BF)
        rhs[2, m] = before(dpre).astype(BF)
        return 0

    lax.fori_loop(0, SECTIONS, redo_back, 0)

    def gradients(core, ref):
        tails = []
        for j in range(2):
            k = 2 * core + j
            term = t_dot(
                lhs[lax.div(k, 3)].reshape(SECTIONS * ROWS, C), rhs[k].reshape(SECTIONS * ROWS, C)
            )
            ref[2 * j * C : (2 * j + 1) * C, :] = term[:, 0:128].astype(ref.dtype)
            ref[(2 * j + 1) * C : (2 * j + 2) * C, :] = term[:, 128:256].astype(ref.dtype)
            tails.append(term[:, 256:320])
        ref[4 * C : 5 * C, :] = jnp.concatenate(tails, 1).astype(ref.dtype)
        ref[5 * C : HALF, :] = jnp.zeros((HALF - 5 * C, 128), ref.dtype)

    gradients(other, sb)
    swap = remote(sb, rb, core_sem.at[0], core_sem.at[1], sibling)
    swap.start()
    gradients(c, gown)
    swap.wait_recv()
    chip[...] = (gown[...] + rb[...].astype(F32)).astype(BF)

    def rows(start, size):
        return pl.ds(pl.multiple_of(start, 16), size)

    def a1(q, to, slot):
        lo, n = CHUNK_A[q]
        return remote(
            chip.at[rows(to * PA + lo, n)], ra.at[slot, pl.ds(lo, n)], a1s.at[q, to], a1r.at[q, slot], at_y(to)
        )

    def b1(q, to, slot):
        lo, n = CHUNK_B[q]
        return remote(
            chip.at[rows(HA + to * PB + lo, n)], rbz.at[slot, pl.ds(lo, n)], b1s.at[q, to], b1r.at[q, slot], at_z(to)
        )

    def a2(q, to, slot):
        ref = ra2.at[slot, pl.ds(*CHUNK_A[q])]
        return remote(ref, ref, a2s.at[q, to], a2r.at[q, slot], at_z(to))

    def b2(q, to, slot):
        ref = rb2.at[slot, pl.ds(*CHUNK_B[q])]
        return remote(ref, ref, b2s.at[q, to], b2r.at[q, slot], at_y(to))

    def a3(q, to, slot):
        lo, n = CHUNK_A[q]
        ref = fin.at[c, rows(slot * PA + lo, n)]
        return remote(ref, ref, a3s.at[q, to], a3r.at[q, slot], at_y(to))

    def b3(q, to, slot):
        lo, n = CHUNK_B[q]
        ref = fin.at[c, rows(HA + slot * PB + lo, n)]
        return remote(ref, ref, b3s.at[q, to], b3r.at[q, slot], at_z(to))

    def total(ref, chunk):
        lo, n = chunk
        value = ref[0, lo : lo + n].astype(F32)
        for i in range(1, 8):
            value = value + ref[i, lo : lo + n].astype(F32)
        return value.astype(BF)

    for q in range(2):

        def first(i):
            a1(q, y_of(i), y).start()
            b1(q, z_of(i), z).start()

        each(Y, first)
    ra[y] = chip[rows(y * PA, PA), :]
    rbz[z] = chip[rows(HA + z * PB, PB), :]
    for q in range(2):
        lo, n = CHUNK_A[q]
        each(Y, lambda i: a1(q, y_of(i), y_of(i)).wait_recv())
        ra2[z, lo : lo + n] = total(ra, (lo, n))
        each(Z, lambda i: a2(q, z_of(i), z).start())
        lo, n = CHUNK_B[q]
        each(Z, lambda i: b1(q, z_of(i), z_of(i)).wait_recv())
        rb2[y, lo : lo + n] = total(rbz, (lo, n))
        each(Y, lambda i: b2(q, y_of(i), y).start())
    for q in range(2):
        lo, n = CHUNK_A[q]
        each(Z, lambda i: a2(q, z_of(i), z_of(i)).wait_recv())
        fin[c, rows(y * PA + lo, n), :] = total(ra2, (lo, n))
        each(Y, lambda i: a3(q, y_of(i), y).start())
        lo, n = CHUNK_B[q]
        each(Y, lambda i: b2(q, y_of(i), y_of(i)).wait_recv())
        fin[c, rows(HA + z * PB + lo, n), :] = total(rb2, (lo, n))
        each(Z, lambda i: b3(q, z_of(i), z).start())

    def end(core, which):
        ref = fin.at[core, pl.ds(HA * which, HB if which else HA)]
        return remote(ref, ref, end_sem.at[0, which], end_sem.at[1, which], sibling)

    for q in range(2):
        each(Y, lambda i: a3(q, y_of(i), y_of(i)).wait_recv())
    end(c, 0).start()
    for q in range(2):
        each(Z, lambda i: b3(q, z_of(i), z_of(i)).wait_recv())
    end(c, 1).start()
    end(other, 0).wait_recv()
    end(other, 1).wait_recv()

    for to in (right, left, far):
        over_x(p, to).wait_send()
    for section in (left, right, far):
        for way in range(4):
            to_next(section, way, color).wait_send()
        for part in range(4):
            to_core(section, c, part).wait_send()
    each(Z, lambda i: z_copy(z_of(i), z).wait_send())
    for kind in range(2):
        each(YL, lambda i: y_copy(kind, yl_of(i), yl).wait_send())

    def left_us(i):
        s = x_of(i)
        remote(hs.at[s], hr.at[p], h_send.at[s], h_recv.at[p], at_x(s)).wait_send()
        remote(ds.at[s], dr.at[p], d_send.at[s], d_recv.at[p], at_x(s)).wait_send()

    each(SECTIONS, left_us)
    swap.wait_send()
    for q in range(2):

        def drained(i):
            a1(q, y_of(i), y).wait_send()
            b1(q, z_of(i), z).wait_send()
            a2(q, z_of(i), z).wait_send()
            b2(q, y_of(i), y).wait_send()
            a3(q, y_of(i), y).wait_send()
            b3(q, z_of(i), z).wait_send()

        each(Y, drained)
    end(c, 0).wait_send()
    end(c, 1).wait_send()


def unpack_kernel(scale, fin, conv_out, out_out):
    for k in range(4):
        ref = conv_out.at[0, k] if k < 3 else out_out.at[0]
        core, j = divmod(k, 2)
        ref[:, 0:128] = fin[core, 2 * j * C : (2 * j + 1) * C, :].astype(F32) * scale
        ref[:, 128:256] = fin[core, (2 * j + 1) * C : (2 * j + 2) * C, :].astype(F32) * scale
        tail = fin[core, 4 * C : 5 * C, :].astype(F32) * scale
        ref[:, 256:320] = tail[:, 64 * j : 64 * j + 64]


def body(video, cotangent, timesteps, conv_weight, out_weight):
    far_memory = pl.BlockSpec(memory_space=pltpu.HBM)
    vmem = pl.BlockSpec(memory_space=pltpu.VMEM)
    dma = pltpu.SemaphoreType.DMA
    stack = (SECTIONS, ROWS, C)
    rows = video.shape[0] * 4 * 64 * video.shape[3]
    packed = pl.pallas_call(
        kernel,
        out_shape=jax.ShapeDtypeStruct((2, HALF, 128), BF),
        in_specs=[far_memory] * 5,
        out_specs=vmem,
        scratch_shapes=[
            pltpu.VMEM((2, 64, C), BF),
            pltpu.VMEM((2, 64, C), BF),
            pltpu.VMEM((1, SECTIONS), jnp.int32),
            pltpu.VMEM((SECTIONS, C), F32),
            pltpu.VMEM((SECTIONS, 8, QUARTER, C), BF),
            pltpu.VMEM((Z, 32, C), BF),
            pltpu.VMEM((Z, 32, C), BF),
            pltpu.VMEM((2, YL, 32, C), BF),
            pltpu.VMEM((2, YL, 32, C), BF),
            pltpu.VMEM(stack, BF),
            pltpu.VMEM(stack, BF),
            pltpu.VMEM(stack, F32),
            pltpu.VMEM(stack, BF),
            pltpu.VMEM((2, *stack), BF),
            pltpu.VMEM((4, *stack), BF),
            pltpu.VMEM((HALF, 128), F32),
            pltpu.VMEM((HALF, 128), BF),
            pltpu.VMEM((HALF, 128), BF),
            pltpu.VMEM((HALF, 128), BF),
            pltpu.VMEM((8, PA, 128), BF),
            pltpu.VMEM((8, PB, 128), BF),
            pltpu.VMEM((8, PA, 128), BF),
            pltpu.VMEM((8, PB, 128), BF),
            dma((5,)),
            dma((Z,)), dma((Z,)), dma((2, YL)), dma((2, YL)),
            dma((SECTIONS,)), dma((SECTIONS,)),
            dma((SECTIONS, 4)), dma((SECTIONS, 4)), dma((SECTIONS, 4)), dma((SECTIONS, 4)),
            dma((SECTIONS,)), dma((SECTIONS,)), dma((SECTIONS,)), dma((SECTIONS,)),
            dma((2,)),
        ]
        + [dma((2, 8))] * 12
        + [dma((2, 2))],
        compiler_params=pltpu.CompilerParams(
            collective_id=1, has_side_effects=True, vmem_limit_bytes=56 << 20
        ),
        name="main",
    )(
        video,
        cotangent,
        timesteps.T,
        conv_weight.reshape(1, 6, QUARTER, C),
        out_weight.reshape(1, 2, QUARTER, C),
    )
    return pl.pallas_call(
        functools.partial(unpack_kernel, 1.0 / math.sqrt(rows)),
        out_shape=(
            jax.ShapeDtypeStruct((1, 3, C, C), F32),
            jax.ShapeDtypeStruct((1, C, C), F32),
        ),
        in_specs=[vmem],
        out_specs=(vmem, vmem),
        name="unpack",
    )(packed)


def solution(mesh):
    return jax.shard_map(
        body,
        mesh=mesh,
        in_specs=(
            P(None, "dp", "tm", None, None),
            P(None, "dp", "tm", None, None),
            P(None, "dp"),
            P("pipe", None, None, None),
            P("pipe", None, None),
        ),
        out_specs=(P("pipe", None, None, None), P("pipe", None, None)),
        check_vma=False,
    )
```

```python
import functools
import math

import jax
import jax.numpy as jnp
from jax import lax
from jax.experimental import pallas as pl
from jax.experimental.pallas import tpu as pltpu
from jax.sharding import PartitionSpec as P

EPSILON = 1e-06
MESH = pl.DeviceIdType.MESH
SECTIONS = 4
C = 320
ROWS = 128
YL, Z, Y = 4, 8, 8
PA, PB = 112, 96
HA, HB = 8 * PA, 8 * PB
HALF = HA + HB
CHUNK_A, CHUNK_B = ((0, 48), (48, 32), (80, 32)), ((0, 32), (32, 32), (64, 32))
CHUNKS = 3
QUARTER = C // 2
BF = jnp.bfloat16
F32 = jnp.float32


def place():
    p, t, d = lax.axis_index("pipe"), lax.axis_index("tm"), lax.axis_index("dp")
    return p, lax.div(d, 2) * YL + lax.div(t, Z), lax.rem(t, Z), lax.rem(d, 2)


def device(p, y, z, c):
    return (p, lax.rem(y, YL) * Z + z, lax.div(y, YL) * 2 + c)


def remote(src, dst, send, recv, to):
    return pltpu.make_async_remote_copy(
        src_ref=src, dst_ref=dst, send_sem=send, recv_sem=recv, device_id=to, device_id_type=MESH
    )


def each(count, fn):
    def step(i, _):
        fn(i)
        return 0

    lax.fori_loop(1, count, step, 0)


def dot(a, b):
    return jnp.dot(a, b, preferred_element_type=F32)


def dot_t(a, b):
    return lax.dot_general(a, b, (((1,), (1,)), ((), ())), preferred_element_type=F32)


def t_dot(a, b):
    return lax.dot_general(a, b, (((0,), (0,)), ((), ())), preferred_element_type=F32)


def normalize(h):
    x = h.astype(F32)
    inv = lax.rsqrt(jnp.mean(x * x, -1, keepdims=True) + EPSILON)
    return x, inv, x * inv


def before(v):
    row = lax.rem(lax.broadcasted_iota(jnp.int32, v.shape, 0), ROWS)
    return jnp.where(row < 2, 0.0, pltpu.roll(v, 2, 0))


def after(v):
    row = lax.rem(lax.broadcasted_iota(jnp.int32, v.shape, 0), ROWS)
    return jnp.where(row >= ROWS - 2, 0.0, pltpu.roll(v, v.shape[0] - 2, 0))


def reorder(source_of, v):
    r = lax.broadcasted_iota(jnp.int32, (ROWS, ROWS), 0)
    k = lax.broadcasted_iota(jnp.int32, (ROWS, ROWS), 1)
    pick = jnp.where(source_of(r) == k, 1.0, 0.0).astype(BF)
    return dot(pick, v).astype(BF)


def to_z(r):
    return lax.rem(lax.div(r, 8), 2) * 64 + lax.div(r, 16) * 8 + lax.rem(r, 8)


def to_y(r):
    return lax.div(lax.rem(r, 32), 2) * 8 + lax.div(r, 32) * 2 + lax.rem(r, 2)


def kernel(
    video, cotangent, times, convw, outw, packed,
    vin, cin, tin, emb, w, s1s, s1d, s2s, s2d, hs, ds, pre_s, hr, lhs, rhs,
    gown, sb, rb, chip, ra, rbz, ra2, rb2, fin,
    in_sem, z_send, z_recv, y_send, y_recv,
    x_send, x_recv, n_send, n_recv, c_send, c_recv,
    h_send, h_recv, d_send, d_recv,
    core_sem, a1s, a1r, b1s, b1r, a2s, a2r, b2s, b2r, a3s, a3r, b3s, b3r, end_sem, out_sem,
):
    p, y, z, c = place()
    yl = lax.rem(y, YL)
    ybase = y - yl
    other = 1 - c
    loads = [
        pltpu.make_async_copy(convw.at[0], w.at[p, pl.ds(0, 6)], in_sem.at[2]),
        pltpu.make_async_copy(outw.at[0], w.at[p, pl.ds(6, 2)], in_sem.at[3]),
        pltpu.make_async_copy(video.at[p, 0], vin, in_sem.at[0]),
        pltpu.make_async_copy(cotangent.at[p, 0], cin, in_sem.at[1]),
        pltpu.make_async_copy(times, tin, in_sem.at[4]),
    ]
    for load in loads:
        load.start()

    barrier = pltpu.get_barrier_semaphore()

    def greet(to):
        pl.semaphore_signal(barrier, inc=1, device_id=to, device_id_type=MESH)

    def at_x(to):
        return device(to, y, z, c)

    def at_y(to):
        return device(p, to, z, c)

    def at_z(to):
        return device(p, y, to, c)

    def x_of(i):
        return lax.rem(p + i, SECTIONS)

    def y_of(i):
        return lax.rem(y + i, Y)

    def z_of(i):
        return lax.rem(z + i, Z)

    sibling = device(p, y, z, other)
    each(SECTIONS, lambda i: greet(at_x(x_of(i))))
    each(Y, lambda i: greet(at_y(y_of(i))))
    each(Z, lambda i: greet(at_z(z_of(i))))
    greet(sibling)
    for load in loads:
        load.wait()
    pl.semaphore_wait(barrier, SECTIONS + Y + Z - 3 + 1)

    color = lax.rem((y + 2 * z) * other + (2 * y + z) * c, 4)
    step_y, step_z = other, c
    nexts = [
        device(p, lax.rem(y + step_y, Y), lax.rem(z + step_z, Z), c),
        device(p, lax.rem(y + Y - step_y, Y), lax.rem(z + Z - step_z, Z), c),
        device(p, lax.rem(y + step_z, Y), lax.rem(z + step_y, Z), c),
        device(p, lax.rem(y + Y - step_z, Y), lax.rem(z + Z - step_y, Z), c),
    ]
    parts = [pl.ds(0, QUARTER), pl.ds(0, QUARTER), pl.ds(0, QUARTER // 2), pl.ds(QUARTER // 2, QUARTER // 2)]
    quarter = [lax.rem(color + k, 4) for k in range(4)]

    def over_x(section, to):
        ref = w.at[section, 4 * c + color]
        return remote(ref, ref, x_send.at[to], x_recv.at[section], at_x(to))

    def to_next(section, way, part):
        ref = w.at[section, 4 * c + part, parts[way]]
        return remote(ref, ref, n_send.at[section, way], n_recv.at[section, way], nexts[way])

    def to_core(section, core, part):
        ref = w.at[section, 4 * core + part]
        return remote(ref, ref, c_send.at[section, part], c_recv.at[section, part], sibling)

    right, left, far = x_of(1), x_of(3), x_of(2)
    first = p == 0
    for to in (jnp.where(first, far, right), jnp.where(first, right, left), jnp.where(first, left, far)):
        over_x(p, to).start()

    s1s[:, 0:16, :] = reorder(to_z, vin[...].reshape(ROWS, C)).reshape(Z, 16, C)
    s1s[:, 16:32, :] = reorder(to_z, cin[...].reshape(ROWS, C)).reshape(Z, 16, C)

    def z_copy(at, slot):
        return remote(s1s.at[at], s1d.at[slot], z_send.at[at], z_recv.at[slot], at_z(at))

    each(Z, lambda i: z_copy(z_of(i), z).start())
    s1d[z] = s1s[z]

    lane = lax.broadcasted_iota(jnp.int32, (1, C), 1)
    index = jnp.where(lane < C // 2, lane, lane - C // 2).astype(F32)
    freq = jnp.exp(index * (-math.log(10000.0) / (C // 2)))
    for m in range(SECTIONS):
        angle = tin[:, m : m + 1].astype(F32) * freq
        emb[m : m + 1, :] = jnp.where(lane < C // 2, jnp.sin(angle), jnp.cos(angle))

    def unless_own(section, fn):
        @pl.when(p != section)
        def _():
            fn(section)

    def spread(section):
        over_x(section, p).wait_recv()
        for way in range(4):
            to_next(section, way, color).start()
        to_core(section, c, color).start()

    def relay(section):
        for way, k in ((0, 3), (1, 1), (2, 2)):
            to_next(section, way, quarter[k]).wait_recv()
            if way == 2:
                to_next(section, 3, quarter[k]).wait_recv()
            to_core(section, c, quarter[k]).start()

    def complete(section):
        for part in range(4):
            to_core(section, other, part).wait_recv()

    unless_own(0, spread)
    unless_own(1, spread)

    each(Z, lambda i: z_copy(z_of(i), z_of(i)).wait_recv())

    def yl_of(i):
        return lax.rem(yl + i, YL)

    def y_copy(kind, at, slot):
        return remote(
            s2s.at[kind, at], s2d.at[kind, slot], y_send.at[kind, at], y_recv.at[kind, slot], at_y(ybase + at)
        )

    for kind in range(2):
        s2s[kind] = reorder(to_y, s1d[:, 16 * kind : 16 * kind + 16, :].reshape(ROWS, C)).reshape(YL, 32, C)
        each(YL, lambda i: y_copy(kind, yl_of(i), yl).start())
        unless_own(2 + kind, spread)
        s2d[kind, yl] = s2s[kind, yl]

    def give(value, kept, send, recv, section):
        copy = remote(value.at[section], kept.at[p], send.at[section], recv.at[p], at_x(section))

        @pl.when(p != section)
        def _():
            copy.start()

        @pl.when(p == section)
        def _():
            kept[p] = value[section]

    dr = rhs.at[3]
    unless_own(0, relay)
    each(YL, lambda i: y_copy(0, yl_of(i), yl_of(i)).wait_recv())
    hs[0] = s2d[0].reshape(ROWS, C)
    give(hs, hr, h_send, h_recv, 0)
    unless_own(1, relay)

    def weight(section, k):
        return w[section, 2 * k : 2 * k + 2].reshape(C, C)

    emb_row = emb[pl.ds(p, 1), :]
    for s in range(SECTIONS):
        unless_own(s, complete)
        x, inv, normed = normalize(hs[s])
        pre = emb_row + dot(before(normed).astype(BF), weight(s, 0))
        pre = pre + dot(normed.astype(BF), weight(s, 1))
        pre = pre + dot(after(normed).astype(BF), weight(s, 2))
        pre_s[s] = pre
        if s + 1 < SECTIONS:
            act = (pre * jax.nn.sigmoid(pre)).astype(BF)
            hs[s + 1] = (x + dot(act, weight(s, 3))).astype(BF)
            give(hs, hr, h_send, h_recv, s + 1)
        if s + 2 < SECTIONS:
            unless_own(s + 2, relay)
        if s == 2:
            each(YL, lambda i: y_copy(1, yl_of(i), yl_of(i)).wait_recv())
            ds[3] = s2d[1].reshape(ROWS, C)
            give(ds, dr, d_send, d_recv, 3)
    for s in (3, 2, 1):
        x, inv, normed = normalize(hs[s])
        grad = ds[s]
        pre = pre_s[s]
        sig = jax.nn.sigmoid(pre)
        dpre = dot_t(grad, weight(s, 3)) * sig * (1.0 + pre * (1.0 - sig))
        dnorm = dot_t(after(dpre).astype(BF), weight(s, 0))
        dnorm = dnorm + dot_t(dpre.astype(BF), weight(s, 1))
        dnorm = dnorm + dot_t(before(dpre).astype(BF), weight(s, 2))
        mean = jnp.mean(dnorm * normed, -1, keepdims=True)
        ds[s - 1] = (grad.astype(F32) + inv * (dnorm - normed * mean)).astype(BF)
        give(ds, dr, d_send, d_recv, s - 1)

    def micro(i):
        return x_of(i + jnp.where(i == 2, 1, 0) - jnp.where(i == 3, 1, 0))

    def taken(kept, value, send, recv, i):
        m = micro(i)

        @pl.when(i > 0)
        def _():
            remote(value.at[0], kept.at[m], send.at[0], recv.at[m], at_x(m)).wait_recv()

        return m

    def redo(i, _):
        m = taken(hr, hs, h_send, h_recv, i)
        x, inv, normed = normalize(hr[m])
        low = normed.astype(BF)
        pre = emb[pl.ds(m, 1), :] + dot(before(normed).astype(BF), weight(p, 0))
        pre = pre + dot(low, weight(p, 1))
        pre = pre + dot(after(normed).astype(BF), weight(p, 2))
        pre_s[m] = pre
        lhs[0, m] = low
        lhs[1, m] = (pre * jax.nn.sigmoid(pre)).astype(BF)
        return 0

    lax.fori_loop(0, SECTIONS, redo, 0)

    def redo_back(i, _):
        m = taken(dr, ds, d_send, d_recv, i)
        pre = pre_s[m]
        sig = jax.nn.sigmoid(pre)
        dpre = dot_t(rhs[3, m], weight(p, 3)) * sig * (1.0 + pre * (1.0 - sig))
        rhs[0, m] = after(dpre).astype(BF)
        rhs[1, m] = dpre.astype(BF)
        rhs[2, m] = before(dpre).astype(BF)
        return 0

    lax.fori_loop(0, SECTIONS, redo_back, 0)

    def gradients(core, ref):
        tails = []
        for j in range(2):
            k = 2 * core + j
            term = t_dot(
                lhs[lax.div(k, 3)].reshape(SECTIONS * ROWS, C), rhs[k].reshape(SECTIONS * ROWS, C)
            )
            ref[2 * j * C : (2 * j + 1) * C, :] = term[:, 0:128].astype(ref.dtype)
            ref[(2 * j + 1) * C : (2 * j + 2) * C, :] = term[:, 128:256].astype(ref.dtype)
            tails.append(term[:, 256:320])
        ref[4 * C : 5 * C, :] = jnp.concatenate(tails, 1).astype(ref.dtype)
        ref[5 * C : HALF, :] = jnp.zeros((HALF - 5 * C, 128), ref.dtype)

    gradients(other, sb)
    swap = remote(sb, rb, core_sem.at[0], core_sem.at[1], sibling)
    swap.start()
    gradients(c, gown)
    swap.wait_recv()
    chip[...] = (gown[...] + rb[...].astype(F32)).astype(BF)

    def rows(start, size):
        return pl.ds(pl.multiple_of(start, 16), size)

    def a1(q, to, slot):
        lo, n = CHUNK_A[q]
        return remote(
            chip.at[rows(to * PA + lo, n)], ra.at[slot, pl.ds(lo, n)], a1s.at[q, to], a1r.at[q, slot], at_y(to)
        )

    def b1(q, to, slot):
        lo, n = CHUNK_B[q]
        return remote(
            chip.at[rows(HA + to * PB + lo, n)], rbz.at[slot, pl.ds(lo, n)], b1s.at[q, to], b1r.at[q, slot], at_z(to)
        )

    def a2(q, to, slot):
        ref = ra2.at[slot, pl.ds(*CHUNK_A[q])]
        return remote(ref, ref, a2s.at[q, to], a2r.at[q, slot], at_z(to))

    def b2(q, to, slot):
        ref = rb2.at[slot, pl.ds(*CHUNK_B[q])]
        return remote(ref, ref, b2s.at[q, to], b2r.at[q, slot], at_y(to))

    def a3(q, to, slot):
        lo, n = CHUNK_A[q]
        ref = fin.at[c, rows(slot * PA + lo, n)]
        return remote(ref, ref, a3s.at[q, to], a3r.at[q, slot], at_y(to))

    def b3(q, to, slot):
        lo, n = CHUNK_B[q]
        ref = fin.at[c, rows(HA + slot * PB + lo, n)]
        return remote(ref, ref, b3s.at[q, to], b3r.at[q, slot], at_z(to))

    def total(ref, chunk):
        lo, n = chunk
        value = ref[0, lo : lo + n].astype(F32)
        for i in range(1, 8):
            value = value + ref[i, lo : lo + n].astype(F32)
        return value.astype(BF)

    for q in range(CHUNKS):

        def first(i):
            a1(q, y_of(i), y).start()
            b1(q, z_of(i), z).start()

        each(Y, first)
    ra[y] = chip[rows(y * PA, PA), :]
    rbz[z] = chip[rows(HA + z * PB, PB), :]
    for q in range(CHUNKS):
        lo, n = CHUNK_A[q]
        each(Y, lambda i: a1(q, y_of(i), y_of(i)).wait_recv())
        ra2[z, lo : lo + n] = total(ra, (lo, n))
        each(Z, lambda i: a2(q, z_of(i), z).start())
        lo, n = CHUNK_B[q]
        each(Z, lambda i: b1(q, z_of(i), z_of(i)).wait_recv())
        rb2[y, lo : lo + n] = total(rbz, (lo, n))
        each(Y, lambda i: b2(q, y_of(i), y).start())
    for q in range(CHUNKS):
        lo, n = CHUNK_A[q]
        each(Z, lambda i: a2(q, z_of(i), z_of(i)).wait_recv())
        fin[c, rows(y * PA + lo, n), :] = total(ra2, (lo, n))
        each(Y, lambda i: a3(q, y_of(i), y).start())
        lo, n = CHUNK_B[q]
        each(Y, lambda i: b2(q, y_of(i), y_of(i)).wait_recv())
        fin[c, rows(HA + z * PB + lo, n), :] = total(rb2, (lo, n))
        each(Z, lambda i: b3(q, z_of(i), z).start())

    def end(core, which):
        ref = fin.at[core, pl.ds(HA * which, HB if which else HA)]
        return remote(ref, ref, end_sem.at[0, which], end_sem.at[1, which], sibling)

    def store(core, which):
        part = pl.ds(HA * which, HB if which else HA)
        return pltpu.make_async_copy(fin.at[core, part], packed.at[core, part], out_sem.at[core, which])

    for q in range(CHUNKS):
        each(Y, lambda i: a3(q, y_of(i), y_of(i)).wait_recv())
    end(c, 0).start()
    store(c, 0).start()
    for q in range(CHUNKS):
        each(Z, lambda i: b3(q, z_of(i), z_of(i)).wait_recv())
    end(c, 1).start()
    store(c, 1).start()
    end(other, 0).wait_recv()
    store(other, 0).start()
    end(other, 1).wait_recv()
    store(other, 1).start()

    for to in (right, left, far):
        over_x(p, to).wait_send()
    for section in (left, right, far):
        for way in range(4):
            to_next(section, way, color).wait_send()
        for part in range(4):
            to_core(section, c, part).wait_send()
    each(Z, lambda i: z_copy(z_of(i), z).wait_send())
    for kind in range(2):
        each(YL, lambda i: y_copy(kind, yl_of(i), yl).wait_send())

    def left_us(i):
        s = x_of(i)
        remote(hs.at[s], hr.at[p], h_send.at[s], h_recv.at[p], at_x(s)).wait_send()
        remote(ds.at[s], dr.at[p], d_send.at[s], d_recv.at[p], at_x(s)).wait_send()

    each(SECTIONS, left_us)
    swap.wait_send()
    for q in range(CHUNKS):

        def drained(i):
            a1(q, y_of(i), y).wait_send()
            b1(q, z_of(i), z).wait_send()
            a2(q, z_of(i), z).wait_send()
            b2(q, y_of(i), y).wait_send()
            a3(q, y_of(i), y).wait_send()
            b3(q, z_of(i), z).wait_send()

        each(Y, drained)
    for which in range(2):
        end(c, which).wait_send()
        store(c, which).wait()
        store(other, which).wait()


def unpack_kernel(scale, packed, conv_out, out_out, fin, full, in_sem, out_sem):
    loads = [pltpu.make_async_copy(packed.at[core], fin.at[core], in_sem.at[core]) for core in range(2)]
    for load in loads:
        load.start()
    stores = []
    for k in range(4):
        core, j = divmod(k, 2)
        if j == 0:
            loads[core].wait()
        full[k, :, 0:128] = fin[core, 2 * j * C : (2 * j + 1) * C, :].astype(F32) * scale
        full[k, :, 128:256] = fin[core, (2 * j + 1) * C : (2 * j + 2) * C, :].astype(F32) * scale
        tail = fin[core, 4 * C : 5 * C, :].astype(F32) * scale
        full[k, :, 256:320] = tail[:, 64 * j : 64 * j + 64]
        to = conv_out.at[0, k] if k < 3 else out_out.at[0]
        stores.append(pltpu.make_async_copy(full.at[k], to, out_sem.at[k]))
        stores[k].start()
    for store in stores:
        store.wait()


def body(video, cotangent, timesteps, conv_weight, out_weight):
    far_memory = pl.BlockSpec(memory_space=pltpu.HBM)
    dma = pltpu.SemaphoreType.DMA
    stack = (SECTIONS, ROWS, C)
    rows = video.shape[0] * 4 * 64 * video.shape[3]
    packed = pl.pallas_call(
        kernel,
        out_shape=jax.ShapeDtypeStruct((2, HALF, 128), BF),
        in_specs=[far_memory] * 5,
        out_specs=far_memory,
        scratch_shapes=[
            pltpu.VMEM((2, 64, C), BF),
            pltpu.VMEM((2, 64, C), BF),
            pltpu.VMEM((1, SECTIONS), jnp.int32),
            pltpu.VMEM((SECTIONS, C), F32),
            pltpu.VMEM((SECTIONS, 8, QUARTER, C), BF),
            pltpu.VMEM((Z, 32, C), BF),
            pltpu.VMEM((Z, 32, C), BF),
            pltpu.VMEM((2, YL, 32, C), BF),
            pltpu.VMEM((2, YL, 32, C), BF),
            pltpu.VMEM(stack, BF),
            pltpu.VMEM(stack, BF),
            pltpu.VMEM(stack, F32),
            pltpu.VMEM(stack, BF),
            pltpu.VMEM((2, *stack), BF),
            pltpu.VMEM((4, *stack), BF),
            pltpu.VMEM((HALF, 128), F32),
            pltpu.VMEM((HALF, 128), BF),
            pltpu.VMEM((HALF, 128), BF),
            pltpu.VMEM((HALF, 128), BF),
            pltpu.VMEM((8, PA, 128), BF),
            pltpu.VMEM((8, PB, 128), BF),
            pltpu.VMEM((8, PA, 128), BF),
            pltpu.VMEM((8, PB, 128), BF),
            pltpu.VMEM((2, HALF, 128), BF),
            dma((5,)),
            dma((Z,)), dma((Z,)), dma((2, YL)), dma((2, YL)),
            dma((SECTIONS,)), dma((SECTIONS,)),
            dma((SECTIONS, 4)), dma((SECTIONS, 4)), dma((SECTIONS, 4)), dma((SECTIONS, 4)),
            dma((SECTIONS,)), dma((SECTIONS,)), dma((SECTIONS,)), dma((SECTIONS,)),
            dma((2,)),
        ]
        + [dma((CHUNKS, 8))] * 12
        + [dma((2, 2))] * 2,
        compiler_params=pltpu.CompilerParams(
            collective_id=1, has_side_effects=True, vmem_limit_bytes=56 << 20
        ),
        name="main",
    )(
        video,
        cotangent,
        timesteps.T,
        conv_weight.reshape(1, 6, QUARTER, C),
        out_weight.reshape(1, 2, QUARTER, C),
    )
    return pl.pallas_call(
        functools.partial(unpack_kernel, 1.0 / math.sqrt(rows)),
        out_shape=(
            jax.ShapeDtypeStruct((1, 3, C, C), F32),
            jax.ShapeDtypeStruct((1, C, C), F32),
        ),
        in_specs=[far_memory],
        out_specs=(far_memory, far_memory),
        scratch_shapes=[
            pltpu.VMEM((2, HALF, 128), BF),
            pltpu.VMEM((4, C, C), F32),
            dma((2,)),
            dma((4,)),
        ],
        compiler_params=pltpu.CompilerParams(vmem_limit_bytes=56 << 20),
        name="unpack",
    )(packed)


def solution(mesh):
    return jax.shard_map(
        body,
        mesh=mesh,
        in_specs=(
            P(None, "dp", "tm", None, None),
            P(None, "dp", "tm", None, None),
            P(None, "dp"),
            P("pipe", None, None, None),
            P("pipe", None, None),
        ),
        out_specs=(P("pipe", None, None, None), P("pipe", None, None)),
        check_vma=False,
    )
```

```python
import functools
import math

import jax
import jax.numpy as jnp
from jax import lax
from jax.experimental import pallas as pl
from jax.experimental.pallas import tpu as pltpu
from jax.sharding import PartitionSpec as P

EPSILON = 1e-06
MESH = pl.DeviceIdType.MESH
SECTIONS = 4
C = 320
ROWS = 128
YL, Z, Y = 4, 8, 8
PA, PB = 112, 96
HA, HB = 8 * PA, 8 * PB
HALF = HA + HB
CHUNK_A, CHUNK_B = ((0, 48), (48, 32), (80, 32)), ((0, 32), (32, 32), (64, 32))
CHUNKS = 3
WIDE = 2 * ROWS + ROWS // 2
QUARTER = C // 2
BF = jnp.bfloat16
F32 = jnp.float32


def place():
    p, t, d = lax.axis_index("pipe"), lax.axis_index("tm"), lax.axis_index("dp")
    return p, lax.div(d, 2) * YL + lax.div(t, Z), lax.rem(t, Z), lax.rem(d, 2)


def device(p, y, z, c):
    return (p, lax.rem(y, YL) * Z + z, lax.div(y, YL) * 2 + c)


def remote(src, dst, send, recv, to):
    return pltpu.make_async_remote_copy(
        src_ref=src, dst_ref=dst, send_sem=send, recv_sem=recv, device_id=to, device_id_type=MESH
    )


def each(count, fn):
    def step(i, _):
        fn(i)
        return 0

    lax.fori_loop(1, count, step, 0)


def dot(a, b):
    return jnp.dot(a, b, preferred_element_type=F32)


def dot_t(a, b):
    return lax.dot_general(a, b, (((1,), (1,)), ((), ())), preferred_element_type=F32)


def t_dot(a, b):
    return lax.dot_general(a, b, (((0,), (0,)), ((), ())), preferred_element_type=F32)


def normalize(h):
    x = h.astype(F32)
    inv = lax.rsqrt(jnp.mean(x * x, -1, keepdims=True) + EPSILON)
    return x, inv, x * inv


def before(v):
    row = lax.rem(lax.broadcasted_iota(jnp.int32, v.shape, 0), ROWS)
    return jnp.where(row < 2, 0.0, pltpu.roll(v, 2, 0))


def after(v):
    row = lax.rem(lax.broadcasted_iota(jnp.int32, v.shape, 0), ROWS)
    return jnp.where(row >= ROWS - 2, 0.0, pltpu.roll(v, v.shape[0] - 2, 0))


def reorder(source_of, v):
    r = lax.broadcasted_iota(jnp.int32, (ROWS, ROWS), 0)
    k = lax.broadcasted_iota(jnp.int32, (ROWS, ROWS), 1)
    pick = jnp.where(source_of(r) == k, 1.0, 0.0).astype(BF)
    return dot(pick, v).astype(BF)


def to_z(r):
    return lax.rem(lax.div(r, 8), 2) * 64 + lax.div(r, 16) * 8 + lax.rem(r, 8)


def to_y(r):
    return lax.div(lax.rem(r, 32), 2) * 8 + lax.div(r, 32) * 2 + lax.rem(r, 2)


def kernel(
    video, cotangent, times, convw, outw, packed,
    vin, cin, tin, emb, w, s1s, s1d, s2s, s2d, hs, ds, slope, dense, hr, dr, lhs, rhs,
    gown, sb, rb, chip, ra, rbz, ra2, rb2, fin,
    in_sem, z_send, z_recv, y_send, y_recv,
    x_send, x_recv, n_send, n_recv, c_send, c_recv,
    h_send, h_recv, d_send, d_recv,
    core_sem, a1s, a1r, b1s, b1r, a2s, a2r, b2s, b2r, a3s, a3r, b3s, b3r, end_sem, out_sem,
):
    p, y, z, c = place()
    yl = lax.rem(y, YL)
    ybase = y - yl
    other = 1 - c
    barrier = pltpu.get_barrier_semaphore()

    def greet(to):
        pl.semaphore_signal(barrier, inc=1, device_id=to, device_id_type=MESH)

    def at_x(to):
        return device(to, y, z, c)

    def at_y(to):
        return device(p, to, z, c)

    def at_z(to):
        return device(p, y, to, c)

    def x_of(i):
        return lax.rem(p + i, SECTIONS)

    def y_of(i):
        return lax.rem(y + i, Y)

    def z_of(i):
        return lax.rem(z + i, Z)

    sibling = device(p, y, z, other)
    for i in (4, 3, 5, 2, 6, 1, 7):
        greet(at_y(y_of(i)))
        greet(at_z(z_of(i)))
    for i in (2, 1, 3):
        greet(at_x(x_of(i)))
    greet(sibling)
    loads = [
        pltpu.make_async_copy(convw.at[0], w.at[p, pl.ds(0, 6)], in_sem.at[2]),
        pltpu.make_async_copy(outw.at[0], w.at[p, pl.ds(6, 2)], in_sem.at[3]),
        pltpu.make_async_copy(video.at[p, 0], vin, in_sem.at[0]),
        pltpu.make_async_copy(cotangent.at[p, 0], cin, in_sem.at[1]),
        pltpu.make_async_copy(times, tin, in_sem.at[4]),
    ]
    for load in loads:
        load.start()

    for load in loads:
        load.wait()

    def by_z(kind, ref):
        s1s[kind] = reorder(to_z, ref[...].reshape(ROWS, C)).reshape(Z, 16, C)

    by_z(0, vin)
    pl.semaphore_wait(barrier, SECTIONS + Y + Z - 3 + 1)

    color = lax.rem((y + 2 * z) * other + (2 * y + z) * c, 4)
    step_y, step_z = other, c
    nexts = [
        device(p, lax.rem(y + step_y, Y), lax.rem(z + step_z, Z), c),
        device(p, lax.rem(y + Y - step_y, Y), lax.rem(z + Z - step_z, Z), c),
        device(p, lax.rem(y + step_z, Y), lax.rem(z + step_y, Z), c),
        device(p, lax.rem(y + Y - step_z, Y), lax.rem(z + Z - step_y, Z), c),
    ]
    parts = [pl.ds(0, QUARTER), pl.ds(0, QUARTER), pl.ds(0, QUARTER // 2), pl.ds(QUARTER // 2, QUARTER // 2)]
    quarter = [lax.rem(color + k, 4) for k in range(4)]

    def over_x(section, to):
        ref = w.at[section, 4 * c + color]
        return remote(ref, ref, x_send.at[to], x_recv.at[section], at_x(to))

    def to_next(section, way, part):
        ref = w.at[section, 4 * c + part, parts[way]]
        return remote(ref, ref, n_send.at[section, way], n_recv.at[section, way], nexts[way])

    def to_core(section, core, part):
        ref = w.at[section, 4 * core + part]
        return remote(ref, ref, c_send.at[section, part], c_recv.at[section, part], sibling)

    right, left, far = x_of(1), x_of(3), x_of(2)
    first = p == 0
    for to in (jnp.where(first, far, right), jnp.where(first, right, left), jnp.where(first, left, far)):
        over_x(p, to).start()

    def z_copy(kind, at, slot):
        return remote(
            s1s.at[kind, at], s1d.at[kind, slot], z_send.at[kind, at], z_recv.at[kind, slot], at_z(at)
        )

    for kind in range(2):
        if kind:
            by_z(1, cin)
        for i in (4, 3, 5, 2, 6, 1, 7):
            z_copy(kind, z_of(i), z).start()
        s1d[kind, z] = s1s[kind, z]

    lane = lax.broadcasted_iota(jnp.int32, (1, C), 1)
    index = jnp.where(lane < C // 2, lane, lane - C // 2).astype(F32)
    freq = jnp.exp(index * (-math.log(10000.0) / (C // 2)))
    for m in range(SECTIONS):
        angle = tin[:, m : m + 1].astype(F32) * freq
        emb[m : m + 1, :] = jnp.where(lane < C // 2, jnp.sin(angle), jnp.cos(angle))

    def unless_own(section, fn):
        @pl.when(p != section)
        def _():
            fn(section)

    def spread(section):
        over_x(section, p).wait_recv()
        for way in range(4):
            to_next(section, way, color).start()
        to_core(section, c, color).start()

    def relay(section):
        for way, k in ((0, 3), (1, 1), (2, 2)):
            to_next(section, way, quarter[k]).wait_recv()
            if way == 2:
                to_next(section, 3, quarter[k]).wait_recv()
            to_core(section, c, quarter[k]).start()

    def complete(section):
        for part in range(4):
            to_core(section, other, part).wait_recv()

    unless_own(0, spread)
    unless_own(1, spread)

    def yl_of(i):
        return lax.rem(yl + i, YL)

    def y_copy(kind, at, slot):
        return remote(
            s2s.at[kind, at], s2d.at[kind, slot], y_send.at[kind, at], y_recv.at[kind, slot], at_y(ybase + at)
        )

    for kind in range(2):
        each(Z, lambda i: z_copy(kind, z_of(i), z_of(i)).wait_recv())
        s2s[kind] = reorder(to_y, s1d[kind].reshape(ROWS, C)).reshape(YL, 32, C)
        if kind:
            unless_own(3, spread)
        each(YL, lambda i: y_copy(kind, yl_of(i), yl).start())
        if not kind:
            unless_own(2, spread)
        s2d[kind, yl] = s2s[kind, yl]

    def give(value, kept, send, recv, section):
        copy = remote(value.at[section], kept.at[p], send.at[section], recv.at[p], at_x(section))

        @pl.when(p != section)
        def _():
            copy.start()

        @pl.when(p == section)
        def _():
            kept[p] = value[section]

    def give_dense(section, value):
        low = value[:, 256:320]
        dense[section, 0:ROWS] = value[:, 0:128].astype(BF)
        dense[section, ROWS : 2 * ROWS] = value[:, 128:256].astype(BF)
        dense[section, 2 * ROWS : WIDE] = jnp.concatenate(
            [low[0 : ROWS // 2], low[ROWS // 2 : ROWS]], 1
        ).astype(BF)
        give(dense, dr, d_send, d_recv, section)

    unless_own(0, relay)
    each(YL, lambda i: y_copy(0, yl_of(i), yl_of(i)).wait_recv())
    hs[0] = s2d[0].reshape(ROWS, C)
    give(hs, hr, h_send, h_recv, 0)
    unless_own(1, relay)

    def weight(section, k):
        return w[section, 2 * k : 2 * k + 2].reshape(C, C)

    emb_row = emb[pl.ds(p, 1), :]
    for s in range(SECTIONS):
        unless_own(s, complete)
        x, inv, normed = normalize(hs[s])
        pre = emb_row + dot(before(normed).astype(BF), weight(s, 0))
        pre = pre + dot(normed.astype(BF), weight(s, 1))
        pre = pre + dot(after(normed).astype(BF), weight(s, 2))
        sig = jax.nn.sigmoid(pre)
        slope[s] = sig * (1.0 + pre * (1.0 - sig))
        if s + 1 < SECTIONS:
            act = (pre * sig).astype(BF)
            hs[s + 1] = (x + dot(act, weight(s, 3))).astype(BF)
            give(hs, hr, h_send, h_recv, s + 1)
        if s + 2 < SECTIONS:
            unless_own(s + 2, relay)
        if s == 2:
            each(YL, lambda i: y_copy(1, yl_of(i), yl_of(i)).wait_recv())
            ds[3] = s2d[1].reshape(ROWS, C)
            give_dense(3, ds[3].astype(F32))
    for s in (3, 2, 1):
        x, inv, normed = normalize(hs[s])
        grad = ds[s]
        dpre = dot_t(grad, weight(s, 3)) * slope[s]
        dnorm = dot_t(after(dpre).astype(BF), weight(s, 0))
        dnorm = dnorm + dot_t(dpre.astype(BF), weight(s, 1))
        dnorm = dnorm + dot_t(before(dpre).astype(BF), weight(s, 2))
        mean = jnp.mean(dnorm * normed, -1, keepdims=True)
        result = grad.astype(F32) + inv * (dnorm - normed * mean)
        give_dense(s - 1, result)
        if s > 1:
            ds[s - 1] = result.astype(BF)

    def micro(i):
        return x_of(i + jnp.where(i == 2, 1, 0) - jnp.where(i == 3, 1, 0))

    def taken(kept, value, send, recv, i):
        m = micro(i)

        @pl.when(i > 0)
        def _():
            remote(value.at[0], kept.at[m], send.at[0], recv.at[m], at_x(m)).wait_recv()

        return m

    def redo(i, _):
        m = taken(hr, hs, h_send, h_recv, i)
        x, inv, normed = normalize(hr[m])
        low = normed.astype(BF)
        pre = emb[pl.ds(m, 1), :] + dot(before(normed).astype(BF), weight(p, 0))
        pre = pre + dot(low, weight(p, 1))
        pre = pre + dot(after(normed).astype(BF), weight(p, 2))
        sig = jax.nn.sigmoid(pre)
        slope[m] = sig * (1.0 + pre * (1.0 - sig))
        lhs[0, m] = low
        lhs[1, m] = (pre * sig).astype(BF)
        return 0

    lax.fori_loop(0, SECTIONS, redo, 0)

    def redo_back(i, _):
        m = taken(dr, dense, d_send, d_recv, i)
        low = dr[m, 2 * ROWS : WIDE].astype(F32)
        low = jnp.concatenate([low[:, 0:64], low[:, 64:128]], 0).astype(BF)
        rhs[3, m, :, 0:128] = dr[m, 0:ROWS]
        rhs[3, m, :, 128:256] = dr[m, ROWS : 2 * ROWS]
        rhs[3, m, :, 256:320] = low
        dpre = dot_t(rhs[3, m], weight(p, 3)) * slope[m]
        rhs[0, m] = after(dpre).astype(BF)
        rhs[1, m] = dpre.astype(BF)
        rhs[2, m] = before(dpre).astype(BF)
        return 0

    lax.fori_loop(0, SECTIONS, redo_back, 0)

    def gradients(core, ref, then):
        tails = []
        for j in range(2):
            k = 2 * core + j
            term = t_dot(
                lhs[lax.div(k, 3)].reshape(SECTIONS * ROWS, C), rhs[k].reshape(SECTIONS * ROWS, C)
            )
            ref[2 * j * C : (2 * j + 1) * C, :] = term[:, 0:128].astype(ref.dtype)
            ref[(2 * j + 1) * C : (2 * j + 2) * C, :] = term[:, 128:256].astype(ref.dtype)
            tails.append(term[:, 256:320])
            if j:
                ref[4 * C : 5 * C, :] = jnp.concatenate(tails, 1).astype(ref.dtype)
                ref[5 * C : HALF, :] = jnp.zeros((HALF - 5 * C, 128), ref.dtype)
            then(j)

    def swap(j):
        part = pl.ds(2 * C * j, HALF - 2 * C if j else 2 * C)
        return remote(sb.at[part], rb.at[part], core_sem.at[0, j], core_sem.at[1, j], sibling)

    gradients(other, sb, lambda j: swap(j).start())
    gradients(c, gown, lambda j: None)
    for j, (lo, hi) in enumerate(((0, 2 * C), (2 * C, HALF))):
        swap(j).wait_recv()
        chip[lo:hi] = (gown[lo:hi] + rb[lo:hi].astype(F32)).astype(BF)

    def rows(start, size):
        return pl.ds(pl.multiple_of(start, 16), size)

    def a1(q, to, slot):
        lo, n = CHUNK_A[q]
        return remote(
            chip.at[rows(to * PA + lo, n)], ra.at[slot, pl.ds(lo, n)], a1s.at[q, to], a1r.at[q, slot], at_y(to)
        )

    def b1(q, to, slot):
        lo, n = CHUNK_B[q]
        return remote(
            chip.at[rows(HA + to * PB + lo, n)], rbz.at[slot, pl.ds(lo, n)], b1s.at[q, to], b1r.at[q, slot], at_z(to)
        )

    def a2(q, to, slot):
        ref = ra2.at[slot, pl.ds(*CHUNK_A[q])]
        return remote(ref, ref, a2s.at[q, to], a2r.at[q, slot], at_z(to))

    def b2(q, to, slot):
        ref = rb2.at[slot, pl.ds(*CHUNK_B[q])]
        return remote(ref, ref, b2s.at[q, to], b2r.at[q, slot], at_y(to))

    def a3(q, to, slot):
        lo, n = CHUNK_A[q]
        ref = fin.at[c, rows(slot * PA + lo, n)]
        return remote(ref, ref, a3s.at[q, to], a3r.at[q, slot], at_y(to))

    def b3(q, to, slot):
        lo, n = CHUNK_B[q]
        ref = fin.at[c, rows(HA + slot * PB + lo, n)]
        return remote(ref, ref, b3s.at[q, to], b3r.at[q, slot], at_z(to))

    def total(ref, chunk):
        lo, n = chunk
        value = ref[0, lo : lo + n].astype(F32)
        for i in range(1, 8):
            value = value + ref[i, lo : lo + n].astype(F32)
        return value.astype(BF)

    for q in range(CHUNKS):

        def first(i):
            a1(q, y_of(i), y).start()
            b1(q, z_of(i), z).start()

        each(Y, first)
    ra[y] = chip[rows(y * PA, PA), :]
    rbz[z] = chip[rows(HA + z * PB, PB), :]
    for q in range(CHUNKS):
        lo, n = CHUNK_A[q]
        each(Y, lambda i: a1(q, y_of(i), y_of(i)).wait_recv())
        ra2[z, lo : lo + n] = total(ra, (lo, n))
        each(Z, lambda i: a2(q, z_of(i), z).start())
        lo, n = CHUNK_B[q]
        each(Z, lambda i: b1(q, z_of(i), z_of(i)).wait_recv())
        rb2[y, lo : lo + n] = total(rbz, (lo, n))
        each(Y, lambda i: b2(q, y_of(i), y).start())
    for q in range(CHUNKS):
        lo, n = CHUNK_A[q]
        each(Z, lambda i: a2(q, z_of(i), z_of(i)).wait_recv())
        fin[c, rows(y * PA + lo, n), :] = total(ra2, (lo, n))
        each(Y, lambda i: a3(q, y_of(i), y).start())
        lo, n = CHUNK_B[q]
        each(Y, lambda i: b2(q, y_of(i), y_of(i)).wait_recv())
        fin[c, rows(HA + z * PB + lo, n), :] = total(rb2, (lo, n))
        each(Z, lambda i: b3(q, z_of(i), z).start())

    def end(core, which):
        ref = fin.at[core, pl.ds(HA * which, HB if which else HA)]
        return remote(ref, ref, end_sem.at[0, which], end_sem.at[1, which], sibling)

    def store(core, which):
        part = pl.ds(HA * which, HB if which else HA)
        return pltpu.make_async_copy(fin.at[core, part], packed.at[core, part], out_sem.at[core, which])

    for q in range(CHUNKS):
        each(Y, lambda i: a3(q, y_of(i), y_of(i)).wait_recv())
    end(c, 0).start()
    store(c, 0).start()
    for q in range(CHUNKS):
        each(Z, lambda i: b3(q, z_of(i), z_of(i)).wait_recv())
    end(c, 1).start()
    store(c, 1).start()
    end(other, 0).wait_recv()
    store(other, 0).start()
    end(other, 1).wait_recv()
    store(other, 1).start()

    for to in (right, left, far):
        over_x(p, to).wait_send()
    for section in (left, right, far):
        for way in range(4):
            to_next(section, way, color).wait_send()
        for part in range(4):
            to_core(section, c, part).wait_send()
    for kind in range(2):
        each(Z, lambda i: z_copy(kind, z_of(i), z).wait_send())
        each(YL, lambda i: y_copy(kind, yl_of(i), yl).wait_send())

    def left_us(i):
        s = x_of(i)
        remote(hs.at[s], hr.at[p], h_send.at[s], h_recv.at[p], at_x(s)).wait_send()
        remote(dense.at[s], dr.at[p], d_send.at[s], d_recv.at[p], at_x(s)).wait_send()

    each(SECTIONS, left_us)
    swap(0).wait_send()
    swap(1).wait_send()
    for q in range(CHUNKS):

        def drained(i):
            a1(q, y_of(i), y).wait_send()
            b1(q, z_of(i), z).wait_send()
            a2(q, z_of(i), z).wait_send()
            b2(q, y_of(i), y).wait_send()
            a3(q, y_of(i), y).wait_send()
            b3(q, z_of(i), z).wait_send()

        each(Y, drained)
    for which in range(2):
        end(c, which).wait_send()
        store(c, which).wait()
        store(other, which).wait()


def unpack_kernel(scale, packed, conv_out, out_out, fin, full, in_sem, out_sem):
    loads = [pltpu.make_async_copy(packed.at[core], fin.at[core], in_sem.at[core]) for core in range(2)]
    for load in loads:
        load.start()
    stores = []
    for k in range(4):
        core, j = divmod(k, 2)
        if j == 0:
            loads[core].wait()
        full[k, :, 0:128] = fin[core, 2 * j * C : (2 * j + 1) * C, :].astype(F32) * scale
        full[k, :, 128:256] = fin[core, (2 * j + 1) * C : (2 * j + 2) * C, :].astype(F32) * scale
        tail = fin[core, 4 * C : 5 * C, :].astype(F32) * scale
        full[k, :, 256:320] = tail[:, 64 * j : 64 * j + 64]
        to = conv_out.at[0, k] if k < 3 else out_out.at[0]
        stores.append(pltpu.make_async_copy(full.at[k], to, out_sem.at[k]))
        stores[k].start()
    for store in stores:
        store.wait()


def body(video, cotangent, timesteps, conv_weight, out_weight):
    far_memory = pl.BlockSpec(memory_space=pltpu.HBM)
    dma = pltpu.SemaphoreType.DMA
    stack = (SECTIONS, ROWS, C)
    rows = video.shape[0] * 4 * 64 * video.shape[3]
    packed = pl.pallas_call(
        kernel,
        out_shape=jax.ShapeDtypeStruct((2, HALF, 128), BF),
        in_specs=[far_memory] * 5,
        out_specs=far_memory,
        scratch_shapes=[
            pltpu.VMEM((2, 64, C), BF),
            pltpu.VMEM((2, 64, C), BF),
            pltpu.VMEM((1, SECTIONS), jnp.int32),
            pltpu.VMEM((SECTIONS, C), F32),
            pltpu.VMEM((SECTIONS, 8, QUARTER, C), BF),
            pltpu.VMEM((2, Z, 16, C), BF),
            pltpu.VMEM((2, Z, 16, C), BF),
            pltpu.VMEM((2, YL, 32, C), BF),
            pltpu.VMEM((2, YL, 32, C), BF),
            pltpu.VMEM(stack, BF),
            pltpu.VMEM(stack, BF),
            pltpu.VMEM(stack, F32),
            pltpu.VMEM((SECTIONS, WIDE, 128), BF),
            pltpu.VMEM(stack, BF),
            pltpu.VMEM((SECTIONS, WIDE, 128), BF),
            pltpu.VMEM((2, *stack), BF),
            pltpu.VMEM((4, *stack), BF),
            pltpu.VMEM((HALF, 128), F32),
            pltpu.VMEM((HALF, 128), BF),
            pltpu.VMEM((HALF, 128), BF),
            pltpu.VMEM((HALF, 128), BF),
            pltpu.VMEM((8, PA, 128), BF),
            pltpu.VMEM((8, PB, 128), BF),
            pltpu.VMEM((8, PA, 128), BF),
            pltpu.VMEM((8, PB, 128), BF),
            pltpu.VMEM((2, HALF, 128), BF),
            dma((5,)),
            dma((2, Z)), dma((2, Z)), dma((2, YL)), dma((2, YL)),
            dma((SECTIONS,)), dma((SECTIONS,)),
            dma((SECTIONS, 4)), dma((SECTIONS, 4)), dma((SECTIONS, 4)), dma((SECTIONS, 4)),
            dma((SECTIONS,)), dma((SECTIONS,)), dma((SECTIONS,)), dma((SECTIONS,)),
            dma((2, 2)),
        ]
        + [dma((CHUNKS, 8))] * 12
        + [dma((2, 2))] * 2,
        compiler_params=pltpu.CompilerParams(
            collective_id=1, has_side_effects=True, vmem_limit_bytes=56 << 20
        ),
        name="main",
    )(
        video,
        cotangent,
        timesteps.T,
        conv_weight.reshape(1, 6, QUARTER, C),
        out_weight.reshape(1, 2, QUARTER, C),
    )
    return pl.pallas_call(
        functools.partial(unpack_kernel, 1.0 / math.sqrt(rows)),
        out_shape=(
            jax.ShapeDtypeStruct((1, 3, C, C), F32),
            jax.ShapeDtypeStruct((1, C, C), F32),
        ),
        in_specs=[far_memory],
        out_specs=(far_memory, far_memory),
        scratch_shapes=[
            pltpu.VMEM((2, HALF, 128), BF),
            pltpu.VMEM((4, C, C), F32),
            dma((2,)),
            dma((4,)),
        ],
        compiler_params=pltpu.CompilerParams(vmem_limit_bytes=56 << 20),
        name="unpack",
    )(packed)


def solution(mesh):
    return jax.shard_map(
        body,
        mesh=mesh,
        in_specs=(
            P(None, "dp", "tm", None, None),
            P(None, "dp", "tm", None, None),
            P(None, "dp"),
            P("pipe", None, None, None),
            P("pipe", None, None),
        ),
        out_specs=(P("pipe", None, None, None), P("pipe", None, None)),
        check_vma=False,
    )
```

```python
import functools
import math

import jax
import jax.numpy as jnp
from jax import lax
from jax.experimental import pallas as pl
from jax.experimental.pallas import tpu as pltpu
from jax.sharding import PartitionSpec as P

EPSILON = 1e-06
MESH = pl.DeviceIdType.MESH
SECTIONS = 4
C = 320
ROWS = 128
YL, Z, Y = 4, 8, 8
PA, PB = 112, 96
HA, HB = 8 * PA, 8 * PB
HALF = HA + HB
CHUNK_A, CHUNK_B = ((0, 48), (48, 32), (80, 32)), ((0, 32), (32, 32), (64, 32))
CHUNKS = 3
WIDE = 2 * ROWS + ROWS // 2
QUARTER = C // 2
BF = jnp.bfloat16
F32 = jnp.float32


def place():
    p, t, d = lax.axis_index("pipe"), lax.axis_index("tm"), lax.axis_index("dp")
    return p, lax.div(d, 2) * YL + lax.div(t, Z), lax.rem(t, Z), lax.rem(d, 2)


def device(p, y, z, c):
    return (p, lax.rem(y, YL) * Z + z, lax.div(y, YL) * 2 + c)


def remote(src, dst, send, recv, to):
    return pltpu.make_async_remote_copy(
        src_ref=src, dst_ref=dst, send_sem=send, recv_sem=recv, device_id=to, device_id_type=MESH
    )


def each(count, fn):
    def step(i, _):
        fn(i)
        return 0

    lax.fori_loop(1, count, step, 0)


def far_first(fn):
    each(8, lambda i: fn(4 + lax.div(i, 2) * (2 * lax.rem(i, 2) - 1)))


def dot(a, b):
    return jnp.dot(a, b, preferred_element_type=F32)


def dot_t(a, b):
    return lax.dot_general(a, b, (((1,), (1,)), ((), ())), preferred_element_type=F32)


def t_dot(a, b):
    return lax.dot_general(a, b, (((0,), (0,)), ((), ())), preferred_element_type=F32)


def normalize(h):
    x = h.astype(F32)
    inv = lax.rsqrt(jnp.mean(x * x, -1, keepdims=True) + EPSILON)
    return x, inv, x * inv


def before(v):
    row = lax.rem(lax.broadcasted_iota(jnp.int32, v.shape, 0), ROWS)
    return jnp.where(row < 2, 0.0, pltpu.roll(v, 2, 0))


def after(v):
    row = lax.rem(lax.broadcasted_iota(jnp.int32, v.shape, 0), ROWS)
    return jnp.where(row >= ROWS - 2, 0.0, pltpu.roll(v, v.shape[0] - 2, 0))


def reorder(source_of, v):
    r = lax.broadcasted_iota(jnp.int32, (ROWS, ROWS), 0)
    k = lax.broadcasted_iota(jnp.int32, (ROWS, ROWS), 1)
    pick = jnp.where(source_of(r) == k, 1.0, 0.0).astype(BF)
    return dot(pick, v).astype(BF)


def to_z(r):
    return lax.rem(lax.div(r, 8), 2) * 64 + lax.div(r, 16) * 8 + lax.rem(r, 8)


def to_y(r):
    return lax.div(lax.rem(r, 32), 2) * 8 + lax.div(r, 32) * 2 + lax.rem(r, 2)


def kernel(
    video, cotangent, times, convw, outw, packed,
    vin, cin, tin, emb, w, s1s, s1d, s2s, s2d, hs, ds, slope, dense, hr, dr, lhs, rhs,
    gown, sb, rb, chip, ra, rbz, ra2, rb2, fin,
    in_sem, z_send, z_recv, y_send, y_recv,
    x_send, x_recv, n_send, n_recv, c_send, c_recv,
    h_send, h_recv, d_send, d_recv,
    core_sem, a1s, a1r, b1s, b1r, a2s, a2r, b2s, b2r, a3s, a3r, b3s, b3r, end_sem, out_sem,
):
    p, y, z, c = place()
    yl = lax.rem(y, YL)
    ybase = y - yl
    other = 1 - c
    barrier = pltpu.get_barrier_semaphore()

    def greet(to):
        pl.semaphore_signal(barrier, inc=1, device_id=to, device_id_type=MESH)

    def at_x(to):
        return device(to, y, z, c)

    def at_y(to):
        return device(p, to, z, c)

    def at_z(to):
        return device(p, y, to, c)

    def x_of(i):
        return lax.rem(p + i, SECTIONS)

    def y_of(i):
        return lax.rem(y + i, Y)

    def z_of(i):
        return lax.rem(z + i, Z)

    sibling = device(p, y, z, other)
    for i in (4, 3, 5, 2, 6, 1, 7):
        greet(at_y(y_of(i)))
        greet(at_z(z_of(i)))
    for i in (2, 1, 3):
        greet(at_x(x_of(i)))
    greet(sibling)
    loads = [
        pltpu.make_async_copy(convw.at[0], w.at[p, pl.ds(0, 6)], in_sem.at[2]),
        pltpu.make_async_copy(outw.at[0], w.at[p, pl.ds(6, 2)], in_sem.at[3]),
        pltpu.make_async_copy(video.at[p, 0], vin, in_sem.at[0]),
        pltpu.make_async_copy(cotangent.at[p, 0], cin, in_sem.at[1]),
        pltpu.make_async_copy(times, tin, in_sem.at[4]),
    ]
    for load in loads:
        load.start()

    for load in loads:
        load.wait()

    def by_z(kind, ref):
        s1s[kind] = reorder(to_z, ref[...].reshape(ROWS, C)).reshape(Z, 16, C)

    by_z(0, vin)
    pl.semaphore_wait(barrier, SECTIONS + Y + Z - 3 + 1)

    color = lax.rem(2 * y + z, 4)
    step_y, step_z = 0, 1
    nexts = [
        device(p, lax.rem(y + step_y, Y), lax.rem(z + step_z, Z), c),
        device(p, lax.rem(y + Y - step_y, Y), lax.rem(z + Z - step_z, Z), c),
        device(p, lax.rem(y + step_z, Y), lax.rem(z + step_y, Z), c),
        device(p, lax.rem(y + Y - step_z, Y), lax.rem(z + Z - step_y, Z), c),
    ]
    parts = [pl.ds(0, QUARTER), pl.ds(0, QUARTER), pl.ds(0, QUARTER // 2), pl.ds(QUARTER // 2, QUARTER // 2)]
    quarter = [lax.rem(color + k, 4) for k in range(4)]

    def over_x(section, to):
        ref = w.at[section, 4 * c + color]
        return remote(ref, ref, x_send.at[to], x_recv.at[section], at_x(to))

    def to_next(section, way, part):
        ref = w.at[section, 4 * c + part, parts[way]]
        return remote(ref, ref, n_send.at[section, way], n_recv.at[section, way], nexts[way])

    def to_core(section, core, part):
        ref = w.at[section, 4 * core + part]
        return remote(ref, ref, c_send.at[section, part], c_recv.at[section, part], sibling)

    right, left, far = x_of(1), x_of(3), x_of(2)
    first = p == 0
    for to in (jnp.where(first, far, right), jnp.where(first, right, left), jnp.where(first, left, far)):
        over_x(p, to).start()

    def z_copy(kind, at, slot):
        return remote(
            s1s.at[kind, at], s1d.at[kind, slot], z_send.at[kind, at], z_recv.at[kind, slot], at_z(at)
        )

    for kind in range(2):
        if kind:
            by_z(1, cin)
        for i in (4, 3, 5, 2, 6, 1, 7):
            z_copy(kind, z_of(i), z).start()
        s1d[kind, z] = s1s[kind, z]

    lane = lax.broadcasted_iota(jnp.int32, (1, C), 1)
    index = jnp.where(lane < C // 2, lane, lane - C // 2).astype(F32)
    freq = jnp.exp(index * (-math.log(10000.0) / (C // 2)))
    for m in range(SECTIONS):
        angle = tin[:, m : m + 1].astype(F32) * freq
        emb[m : m + 1, :] = jnp.where(lane < C // 2, jnp.sin(angle), jnp.cos(angle))

    def unless_own(section, fn):
        @pl.when(p != section)
        def _():
            fn(section)

    def spread(section):
        over_x(section, p).wait_recv()
        for way in range(4):
            to_next(section, way, color).start()
        to_core(section, c, color).start()

    def relay(section):
        for way, k in ((0, 3), (1, 1), (2, 2)):
            to_next(section, way, quarter[k]).wait_recv()
            if way == 2:
                to_next(section, 3, quarter[k]).wait_recv()
            to_core(section, c, quarter[k]).start()

    def complete(section):
        for part in range(4):
            to_core(section, other, part).wait_recv()

    unless_own(0, spread)
    unless_own(1, spread)

    def yl_of(i):
        return lax.rem(yl + i, YL)

    def y_copy(kind, at, slot):
        return remote(
            s2s.at[kind, at], s2d.at[kind, slot], y_send.at[kind, at], y_recv.at[kind, slot], at_y(ybase + at)
        )

    for kind in range(2):
        if kind:
            unless_own(3, spread)
        each(Z, lambda i: z_copy(kind, z_of(i), z_of(i)).wait_recv())
        s2s[kind] = reorder(to_y, s1d[kind].reshape(ROWS, C)).reshape(YL, 32, C)
        each(YL, lambda i: y_copy(kind, yl_of(i), yl).start())
        if not kind:
            unless_own(2, spread)
        s2d[kind, yl] = s2s[kind, yl]

    def give(value, kept, send, recv, section):
        copy = remote(value.at[section], kept.at[p], send.at[section], recv.at[p], at_x(section))

        @pl.when(p != section)
        def _():
            copy.start()

        @pl.when(p == section)
        def _():
            kept[p] = value[section]

    def give_dense(section, value):
        low = value[:, 256:320]
        dense[section, 0:ROWS] = value[:, 0:128].astype(BF)
        dense[section, ROWS : 2 * ROWS] = value[:, 128:256].astype(BF)
        dense[section, 2 * ROWS : WIDE] = jnp.concatenate(
            [low[0 : ROWS // 2], low[ROWS // 2 : ROWS]], 1
        ).astype(BF)
        give(dense, dr, d_send, d_recv, section)

    unless_own(0, relay)
    each(YL, lambda i: y_copy(0, yl_of(i), yl_of(i)).wait_recv())
    hs[0] = s2d[0].reshape(ROWS, C)
    give(hs, hr, h_send, h_recv, 0)
    unless_own(1, relay)

    def weight(section, k):
        return w[section, 2 * k : 2 * k + 2].reshape(C, C)

    emb_row = emb[pl.ds(p, 1), :]
    for s in range(SECTIONS):
        unless_own(s, complete)
        x, inv, normed = normalize(hs[s])
        pre = emb_row + dot(before(normed).astype(BF), weight(s, 0))
        pre = pre + dot(normed.astype(BF), weight(s, 1))
        pre = pre + dot(after(normed).astype(BF), weight(s, 2))
        sig = jax.nn.sigmoid(pre)
        slope[s] = sig * (1.0 + pre * (1.0 - sig))
        if s + 1 < SECTIONS:
            act = (pre * sig).astype(BF)
            hs[s + 1] = (x + dot(act, weight(s, 3))).astype(BF)
            give(hs, hr, h_send, h_recv, s + 1)
        if s + 2 < SECTIONS:
            unless_own(s + 2, relay)
        if s == 2:
            each(YL, lambda i: y_copy(1, yl_of(i), yl_of(i)).wait_recv())
            ds[3] = s2d[1].reshape(ROWS, C)
            give_dense(3, ds[3].astype(F32))
    for s in (3, 2, 1):
        x, inv, normed = normalize(hs[s])
        grad = ds[s]
        dpre = dot_t(grad, weight(s, 3)) * slope[s]
        dnorm = dot_t(after(dpre).astype(BF), weight(s, 0))
        dnorm = dnorm + dot_t(dpre.astype(BF), weight(s, 1))
        dnorm = dnorm + dot_t(before(dpre).astype(BF), weight(s, 2))
        mean = jnp.mean(dnorm * normed, -1, keepdims=True)
        result = grad.astype(F32) + inv * (dnorm - normed * mean)
        give_dense(s - 1, result)
        if s > 1:
            ds[s - 1] = result.astype(BF)

    def micro(i):
        return x_of(i + jnp.where(i == 2, 1, 0) - jnp.where(i == 3, 1, 0))

    def taken(kept, value, send, recv, i):
        m = micro(i)

        @pl.when(i > 0)
        def _():
            remote(value.at[0], kept.at[m], send.at[0], recv.at[m], at_x(m)).wait_recv()

        return m

    def redo(i, _):
        m = taken(hr, hs, h_send, h_recv, i)
        x, inv, normed = normalize(hr[m])
        low = normed.astype(BF)
        pre = emb[pl.ds(m, 1), :] + dot(before(normed).astype(BF), weight(p, 0))
        pre = pre + dot(low, weight(p, 1))
        pre = pre + dot(after(normed).astype(BF), weight(p, 2))
        sig = jax.nn.sigmoid(pre)
        slope[m] = sig * (1.0 + pre * (1.0 - sig))
        lhs[0, m] = low
        lhs[1, m] = (pre * sig).astype(BF)
        return 0

    lax.fori_loop(0, SECTIONS, redo, 0)

    def redo_back(i, _):
        m = taken(dr, dense, d_send, d_recv, i)
        low = dr[m, 2 * ROWS : WIDE].astype(F32)
        low = jnp.concatenate([low[:, 0:64], low[:, 64:128]], 0).astype(BF)
        rhs[3, m, :, 0:128] = dr[m, 0:ROWS]
        rhs[3, m, :, 128:256] = dr[m, ROWS : 2 * ROWS]
        rhs[3, m, :, 256:320] = low
        dpre = dot_t(rhs[3, m], weight(p, 3)) * slope[m]
        rhs[0, m] = after(dpre).astype(BF)
        rhs[1, m] = dpre.astype(BF)
        rhs[2, m] = before(dpre).astype(BF)
        return 0

    lax.fori_loop(0, SECTIONS, redo_back, 0)

    def gradients(core, ref, then):
        tails = []
        for j in range(2):
            k = 2 * core + j
            term = t_dot(
                lhs[lax.div(k, 3)].reshape(SECTIONS * ROWS, C), rhs[k].reshape(SECTIONS * ROWS, C)
            )
            ref[2 * j * C : (2 * j + 1) * C, :] = term[:, 0:128].astype(ref.dtype)
            ref[(2 * j + 1) * C : (2 * j + 2) * C, :] = term[:, 128:256].astype(ref.dtype)
            tails.append(term[:, 256:320])
            if j:
                ref[4 * C : 5 * C, :] = jnp.concatenate(tails, 1).astype(ref.dtype)
                ref[5 * C : HALF, :] = jnp.zeros((HALF - 5 * C, 128), ref.dtype)
            then(j)

    def swap(j):
        part = pl.ds(2 * C * j, HALF - 2 * C if j else 2 * C)
        return remote(sb.at[part], rb.at[part], core_sem.at[0, j], core_sem.at[1, j], sibling)

    gradients(other, sb, lambda j: swap(j).start())
    gradients(c, gown, lambda j: None)
    for j, (lo, hi) in enumerate(((0, 2 * C), (2 * C, HALF))):
        swap(j).wait_recv()
        chip[lo:hi] = (gown[lo:hi] + rb[lo:hi].astype(F32)).astype(BF)

    def rows(start, size):
        return pl.ds(pl.multiple_of(start, 16), size)

    def a1(q, to, slot):
        lo, n = CHUNK_A[q]
        return remote(
            chip.at[rows(to * PA + lo, n)], ra.at[slot, pl.ds(lo, n)], a1s.at[q, to], a1r.at[q, slot], at_y(to)
        )

    def b1(q, to, slot):
        lo, n = CHUNK_B[q]
        return remote(
            chip.at[rows(HA + to * PB + lo, n)], rbz.at[slot, pl.ds(lo, n)], b1s.at[q, to], b1r.at[q, slot], at_z(to)
        )

    def a2(q, to, slot):
        ref = ra2.at[slot, pl.ds(*CHUNK_A[q])]
        return remote(ref, ref, a2s.at[q, to], a2r.at[q, slot], at_z(to))

    def b2(q, to, slot):
        ref = rb2.at[slot, pl.ds(*CHUNK_B[q])]
        return remote(ref, ref, b2s.at[q, to], b2r.at[q, slot], at_y(to))

    def a3(q, to, slot):
        lo, n = CHUNK_A[q]
        ref = fin.at[c, rows(slot * PA + lo, n)]
        return remote(ref, ref, a3s.at[q, to], a3r.at[q, slot], at_y(to))

    def b3(q, to, slot):
        lo, n = CHUNK_B[q]
        ref = fin.at[c, rows(HA + slot * PB + lo, n)]
        return remote(ref, ref, b3s.at[q, to], b3r.at[q, slot], at_z(to))

    def total(ref, chunk):
        lo, n = chunk
        value = ref[0, lo : lo + n].astype(F32)
        for i in range(1, 8):
            value = value + ref[i, lo : lo + n].astype(F32)
        return value.astype(BF)

    for q in range(CHUNKS):

        def first(i):
            a1(q, y_of(i), y).start()
            b1(q, z_of(i), z).start()

        far_first(first)
    ra[y] = chip[rows(y * PA, PA), :]
    rbz[z] = chip[rows(HA + z * PB, PB), :]
    for q in range(CHUNKS):
        lo, n = CHUNK_A[q]
        each(Y, lambda i: a1(q, y_of(i), y_of(i)).wait_recv())
        ra2[z, lo : lo + n] = total(ra, (lo, n))
        far_first(lambda i: a2(q, z_of(i), z).start())
        lo, n = CHUNK_B[q]
        each(Z, lambda i: b1(q, z_of(i), z_of(i)).wait_recv())
        rb2[y, lo : lo + n] = total(rbz, (lo, n))
        far_first(lambda i: b2(q, y_of(i), y).start())
    for q in range(CHUNKS):
        lo, n = CHUNK_A[q]
        each(Z, lambda i: a2(q, z_of(i), z_of(i)).wait_recv())
        fin[c, rows(y * PA + lo, n), :] = total(ra2, (lo, n))
        far_first(lambda i: a3(q, y_of(i), y).start())
        lo, n = CHUNK_B[q]
        each(Y, lambda i: b2(q, y_of(i), y_of(i)).wait_recv())
        fin[c, rows(HA + z * PB + lo, n), :] = total(rb2, (lo, n))
        far_first(lambda i: b3(q, z_of(i), z).start())

    def end(core, which):
        ref = fin.at[core, pl.ds(HA * which, HB if which else HA)]
        return remote(ref, ref, end_sem.at[0, which], end_sem.at[1, which], sibling)

    def store(core, which):
        part = pl.ds(HA * which, HB if which else HA)
        return pltpu.make_async_copy(fin.at[core, part], packed.at[core, part], out_sem.at[core, which])

    for q in range(CHUNKS):
        each(Y, lambda i: a3(q, y_of(i), y_of(i)).wait_recv())
    end(c, 0).start()
    store(c, 0).start()
    for q in range(CHUNKS):
        each(Z, lambda i: b3(q, z_of(i), z_of(i)).wait_recv())
    end(c, 1).start()
    store(c, 1).start()
    end(other, 0).wait_recv()
    store(other, 0).start()
    end(other, 1).wait_recv()
    store(other, 1).start()

    for to in (right, left, far):
        over_x(p, to).wait_send()
    for section in (left, right, far):
        for way in range(4):
            to_next(section, way, color).wait_send()
        for part in range(4):
            to_core(section, c, part).wait_send()
    for kind in range(2):
        each(Z, lambda i: z_copy(kind, z_of(i), z).wait_send())
        each(YL, lambda i: y_copy(kind, yl_of(i), yl).wait_send())

    def left_us(i):
        s = x_of(i)
        remote(hs.at[s], hr.at[p], h_send.at[s], h_recv.at[p], at_x(s)).wait_send()
        remote(dense.at[s], dr.at[p], d_send.at[s], d_recv.at[p], at_x(s)).wait_send()

    each(SECTIONS, left_us)
    swap(0).wait_send()
    swap(1).wait_send()
    for q in range(CHUNKS):

        def drained(i):
            a1(q, y_of(i), y).wait_send()
            b1(q, z_of(i), z).wait_send()
            a2(q, z_of(i), z).wait_send()
            b2(q, y_of(i), y).wait_send()
            a3(q, y_of(i), y).wait_send()
            b3(q, z_of(i), z).wait_send()

        each(Y, drained)
    for which in range(2):
        end(c, which).wait_send()
        store(c, which).wait()
        store(other, which).wait()


def unpack_kernel(scale, packed, conv_out, out_out, fin, full, in_sem, out_sem):
    loads = [pltpu.make_async_copy(packed.at[core], fin.at[core], in_sem.at[core]) for core in range(2)]
    for load in loads:
        load.start()
    stores = []
    for k in range(4):
        core, j = divmod(k, 2)
        if j == 0:
            loads[core].wait()
        full[k, :, 0:128] = fin[core, 2 * j * C : (2 * j + 1) * C, :].astype(F32) * scale
        full[k, :, 128:256] = fin[core, (2 * j + 1) * C : (2 * j + 2) * C, :].astype(F32) * scale
        tail = fin[core, 4 * C : 5 * C, :].astype(F32) * scale
        full[k, :, 256:320] = tail[:, 64 * j : 64 * j + 64]
        to = conv_out.at[0, k] if k < 3 else out_out.at[0]
        stores.append(pltpu.make_async_copy(full.at[k], to, out_sem.at[k]))
        stores[k].start()
    for store in stores:
        store.wait()


def body(video, cotangent, timesteps, conv_weight, out_weight):
    far_memory = pl.BlockSpec(memory_space=pltpu.HBM)
    dma = pltpu.SemaphoreType.DMA
    stack = (SECTIONS, ROWS, C)
    rows = video.shape[0] * 4 * 64 * video.shape[3]
    packed = pl.pallas_call(
        kernel,
        out_shape=jax.ShapeDtypeStruct((2, HALF, 128), BF),
        in_specs=[far_memory] * 5,
        out_specs=far_memory,
        scratch_shapes=[
            pltpu.VMEM((2, 64, C), BF),
            pltpu.VMEM((2, 64, C), BF),
            pltpu.VMEM((1, SECTIONS), jnp.int32),
            pltpu.VMEM((SECTIONS, C), F32),
            pltpu.VMEM((SECTIONS, 8, QUARTER, C), BF),
            pltpu.VMEM((2, Z, 16, C), BF),
            pltpu.VMEM((2, Z, 16, C), BF),
            pltpu.VMEM((2, YL, 32, C), BF),
            pltpu.VMEM((2, YL, 32, C), BF),
            pltpu.VMEM(stack, BF),
            pltpu.VMEM(stack, BF),
            pltpu.VMEM(stack, F32),
            pltpu.VMEM((SECTIONS, WIDE, 128), BF),
            pltpu.VMEM(stack, BF),
            pltpu.VMEM((SECTIONS, WIDE, 128), BF),
            pltpu.VMEM((2, *stack), BF),
            pltpu.VMEM((4, *stack), BF),
            pltpu.VMEM((HALF, 128), F32),
            pltpu.VMEM((HALF, 128), BF),
            pltpu.VMEM((HALF, 128), BF),
            pltpu.VMEM((HALF, 128), BF),
            pltpu.VMEM((8, PA, 128), BF),
            pltpu.VMEM((8, PB, 128), BF),
            pltpu.VMEM((8, PA, 128), BF),
            pltpu.VMEM((8, PB, 128), BF),
            pltpu.VMEM((2, HALF, 128), BF),
            dma((5,)),
            dma((2, Z)), dma((2, Z)), dma((2, YL)), dma((2, YL)),
            dma((SECTIONS,)), dma((SECTIONS,)),
            dma((SECTIONS, 4)), dma((SECTIONS, 4)), dma((SECTIONS, 4)), dma((SECTIONS, 4)),
            dma((SECTIONS,)), dma((SECTIONS,)), dma((SECTIONS,)), dma((SECTIONS,)),
            dma((2, 2)),
        ]
        + [dma((CHUNKS, 8))] * 12
        + [dma((2, 2))] * 2,
        compiler_params=pltpu.CompilerParams(
            collective_id=1, has_side_effects=True, vmem_limit_bytes=56 << 20
        ),
        name="main",
    )(
        video,
        cotangent,
        timesteps.T,
        conv_weight.reshape(1, 6, QUARTER, C),
        out_weight.reshape(1, 2, QUARTER, C),
    )
    return pl.pallas_call(
        functools.partial(unpack_kernel, 1.0 / math.sqrt(rows)),
        out_shape=(
            jax.ShapeDtypeStruct((1, 3, C, C), F32),
            jax.ShapeDtypeStruct((1, C, C), F32),
        ),
        in_specs=[far_memory],
        out_specs=(far_memory, far_memory),
        scratch_shapes=[
            pltpu.VMEM((2, HALF, 128), BF),
            pltpu.VMEM((4, C, C), F32),
            dma((2,)),
            dma((4,)),
        ],
        compiler_params=pltpu.CompilerParams(vmem_limit_bytes=56 << 20),
        name="unpack",
    )(packed)


def solution(mesh):
    return jax.shard_map(
        body,
        mesh=mesh,
        in_specs=(
            P(None, "dp", "tm", None, None),
            P(None, "dp", "tm", None, None),
            P(None, "dp"),
            P("pipe", None, None, None),
            P("pipe", None, None),
        ),
        out_specs=(P("pipe", None, None, None), P("pipe", None, None)),
        check_vma=False,
    )
```

```python
import functools
import math

import jax
import jax.numpy as jnp
from jax import lax
from jax.experimental import pallas as pl
from jax.experimental.pallas import tpu as pltpu
from jax.sharding import PartitionSpec as P

EPSILON = 1e-06
MESH = pl.DeviceIdType.MESH
SECTIONS = 4
C = 320
ROWS = 128
YL, Z, Y = 4, 8, 8
PA, PB = 112, 96
HA, HB = 8 * PA, 8 * PB
HALF = HA + HB
CHUNK_A, CHUNK_B = ((0, 48), (48, 32), (80, 32)), ((0, 32), (32, 32), (64, 32))
CHUNKS = 3
WIDE = 2 * ROWS + ROWS // 2
QUARTER = C // 2
BF = jnp.bfloat16
F32 = jnp.float32


def place():
    p, t, d = lax.axis_index("pipe"), lax.axis_index("tm"), lax.axis_index("dp")
    return p, lax.div(d, 2) * YL + lax.div(t, Z), lax.rem(t, Z), lax.rem(d, 2)


def device(p, y, z, c):
    return (p, lax.rem(y, YL) * Z + z, lax.div(y, YL) * 2 + c)


def remote(src, dst, send, recv, to):
    return pltpu.make_async_remote_copy(
        src_ref=src, dst_ref=dst, send_sem=send, recv_sem=recv, device_id=to, device_id_type=MESH
    )


def each(count, fn):
    def step(i, _):
        fn(i)
        return 0

    lax.fori_loop(1, count, step, 0)


def far_first(fn):
    each(8, lambda i: fn(4 + lax.div(i, 2) * (2 * lax.rem(i, 2) - 1)))


def dot(a, b):
    return jnp.dot(a, b, preferred_element_type=F32)


def dot_t(a, b):
    return lax.dot_general(a, b, (((1,), (1,)), ((), ())), preferred_element_type=F32)


def t_dot(a, b):
    return lax.dot_general(a, b, (((0,), (0,)), ((), ())), preferred_element_type=F32)


def normalize(h):
    x = h.astype(F32)
    inv = lax.rsqrt(jnp.mean(x * x, -1, keepdims=True) + EPSILON)
    return x, inv, x * inv


def before(v):
    row = lax.rem(lax.broadcasted_iota(jnp.int32, v.shape, 0), ROWS)
    return jnp.where(row < 2, 0.0, pltpu.roll(v, 2, 0))


def after(v):
    row = lax.rem(lax.broadcasted_iota(jnp.int32, v.shape, 0), ROWS)
    return jnp.where(row >= ROWS - 2, 0.0, pltpu.roll(v, v.shape[0] - 2, 0))


def reorder(source_of, v):
    r = lax.broadcasted_iota(jnp.int32, (ROWS, ROWS), 0)
    k = lax.broadcasted_iota(jnp.int32, (ROWS, ROWS), 1)
    pick = jnp.where(source_of(r) == k, 1.0, 0.0).astype(BF)
    return dot(pick, v).astype(BF)


def to_z(r):
    return lax.rem(lax.div(r, 8), 2) * 64 + lax.div(r, 16) * 8 + lax.rem(r, 8)


def to_y(r):
    return lax.div(lax.rem(r, 32), 2) * 8 + lax.div(r, 32) * 2 + lax.rem(r, 2)


def kernel(
    video, cotangent, times, convw, outw, packed,
    vin, cin, tin, emb, w, s1s, s1d, s2s, s2d, hs, ds, slope, dense, packed_h, hr, dr, lhs, rhs,
    gown, sb, rb, chip, ra, rbz, ra2, rb2, fin,
    in_sem, z_send, z_recv, y_send, y_recv,
    x_send, x_recv, n_send, n_recv, c_send, c_recv,
    h_send, h_recv, d_send, d_recv,
    core_sem, a1s, a1r, b1s, b1r, a2s, a2r, b2s, b2r, a3s, a3r, b3s, b3r, end_sem, out_sem,
):
    p, y, z, c = place()
    yl = lax.rem(y, YL)
    ybase = y - yl
    other = 1 - c
    barrier = pltpu.get_barrier_semaphore()

    def greet(to):
        pl.semaphore_signal(barrier, inc=1, device_id=to, device_id_type=MESH)

    def at_x(to):
        return device(to, y, z, c)

    def at_y(to):
        return device(p, to, z, c)

    def at_z(to):
        return device(p, y, to, c)

    def x_of(i):
        return lax.rem(p + i, SECTIONS)

    def y_of(i):
        return lax.rem(y + i, Y)

    def z_of(i):
        return lax.rem(z + i, Z)

    sibling = device(p, y, z, other)
    for i in (4, 3, 5, 2, 6, 1, 7):
        greet(at_y(y_of(i)))
        greet(at_z(z_of(i)))
    for i in (2, 1, 3):
        greet(at_x(x_of(i)))
    greet(sibling)
    loads = [
        pltpu.make_async_copy(convw.at[0], w.at[p, pl.ds(0, 6)], in_sem.at[2]),
        pltpu.make_async_copy(outw.at[0], w.at[p, pl.ds(6, 2)], in_sem.at[3]),
        pltpu.make_async_copy(video.at[p, 0], vin, in_sem.at[0]),
        pltpu.make_async_copy(cotangent.at[p, 0], cin, in_sem.at[1]),
        pltpu.make_async_copy(times, tin, in_sem.at[4]),
    ]
    for load in loads:
        load.start()

    for load in loads:
        load.wait()

    def by_z(kind, ref):
        s1s[kind] = reorder(to_z, ref[...].reshape(ROWS, C)).reshape(Z, 16, C)

    by_z(0, vin)
    pl.semaphore_wait(barrier, SECTIONS + Y + Z - 3 + 1)

    color = lax.rem(2 * y + z, 4)
    step_y, step_z = 0, 1
    nexts = [
        device(p, lax.rem(y + step_y, Y), lax.rem(z + step_z, Z), c),
        device(p, lax.rem(y + Y - step_y, Y), lax.rem(z + Z - step_z, Z), c),
        device(p, lax.rem(y + step_z, Y), lax.rem(z + step_y, Z), c),
        device(p, lax.rem(y + Y - step_z, Y), lax.rem(z + Z - step_y, Z), c),
    ]
    parts = [pl.ds(0, QUARTER), pl.ds(0, QUARTER), pl.ds(0, QUARTER // 2), pl.ds(QUARTER // 2, QUARTER // 2)]
    quarter = [lax.rem(color + k, 4) for k in range(4)]

    def over_x(section, to):
        ref = w.at[section, 4 * c + color]
        return remote(ref, ref, x_send.at[to], x_recv.at[section], at_x(to))

    def to_next(section, way, part):
        ref = w.at[section, 4 * c + part, parts[way]]
        return remote(ref, ref, n_send.at[section, way], n_recv.at[section, way], nexts[way])

    def to_core(section, core, part):
        ref = w.at[section, 4 * core + part]
        return remote(ref, ref, c_send.at[section, part], c_recv.at[section, part], sibling)

    right, left, far = x_of(1), x_of(3), x_of(2)
    first = p == 0
    for to in (jnp.where(first, far, right), jnp.where(first, right, left), jnp.where(first, left, far)):
        over_x(p, to).start()

    def z_copy(kind, at, slot):
        return remote(
            s1s.at[kind, at], s1d.at[kind, slot], z_send.at[kind, at], z_recv.at[kind, slot], at_z(at)
        )

    for kind in range(2):
        if kind:
            by_z(1, cin)
        for i in (4, 3, 5, 2, 6, 1, 7):
            z_copy(kind, z_of(i), z).start()
        s1d[kind, z] = s1s[kind, z]

    lane = lax.broadcasted_iota(jnp.int32, (1, C), 1)
    index = jnp.where(lane < C // 2, lane, lane - C // 2).astype(F32)
    freq = jnp.exp(index * (-math.log(10000.0) / (C // 2)))
    for m in range(SECTIONS):
        angle = tin[:, m : m + 1].astype(F32) * freq
        emb[m : m + 1, :] = jnp.where(lane < C // 2, jnp.sin(angle), jnp.cos(angle))

    def unless_own(section, fn):
        @pl.when(p != section)
        def _():
            fn(section)

    def spread(section):
        over_x(section, p).wait_recv()
        for way in range(4):
            to_next(section, way, color).start()
        to_core(section, c, color).start()

    def relay(section):
        for way, k in ((0, 3), (1, 1), (2, 2)):
            to_next(section, way, quarter[k]).wait_recv()
            if way == 2:
                to_next(section, 3, quarter[k]).wait_recv()
            to_core(section, c, quarter[k]).start()

    def complete(section):
        for part in range(4):
            to_core(section, other, part).wait_recv()

    unless_own(0, spread)
    unless_own(1, spread)

    def yl_of(i):
        return lax.rem(yl + i, YL)

    def y_copy(kind, at, slot):
        return remote(
            s2s.at[kind, at], s2d.at[kind, slot], y_send.at[kind, at], y_recv.at[kind, slot], at_y(ybase + at)
        )

    for kind in range(2):
        if kind:
            unless_own(3, spread)
        each(Z, lambda i: z_copy(kind, z_of(i), z_of(i)).wait_recv())
        s2s[kind] = reorder(to_y, s1d[kind].reshape(ROWS, C)).reshape(YL, 32, C)
        each(YL, lambda i: y_copy(kind, yl_of(i), yl).start())
        if not kind:
            unless_own(2, spread)
        s2d[kind, yl] = s2s[kind, yl]

    def give(value, kept, send, recv, section):
        copy = remote(value.at[section], kept.at[p], send.at[section], recv.at[p], at_x(section))

        @pl.when(p != section)
        def _():
            copy.start()

        @pl.when(p == section)
        def _():
            kept[p] = value[section]

    def pack(ref, section, value):
        low = value[:, 256:320]
        ref[section, 0:ROWS] = value[:, 0:128].astype(BF)
        ref[section, ROWS : 2 * ROWS] = value[:, 128:256].astype(BF)
        ref[section, 2 * ROWS : WIDE] = jnp.concatenate(
            [low[0 : ROWS // 2], low[ROWS // 2 : ROWS]], 1
        ).astype(BF)

    def give_dense(section, value):
        pack(dense, section, value)
        give(dense, dr, d_send, d_recv, section)

    def give_hidden(section, value):
        pack(packed_h, section, value)
        give(packed_h, hr, h_send, h_recv, section)

    unless_own(0, relay)
    each(YL, lambda i: y_copy(0, yl_of(i), yl_of(i)).wait_recv())
    hs[0] = s2d[0].reshape(ROWS, C)
    give_hidden(0, hs[0].astype(F32))
    unless_own(1, relay)

    def weight(section, k):
        return w[section, 2 * k : 2 * k + 2].reshape(C, C)

    emb_row = emb[pl.ds(p, 1), :]
    for s in range(SECTIONS):
        unless_own(s, complete)
        x, inv, normed = normalize(hs[s])
        pre = emb_row + dot(before(normed).astype(BF), weight(s, 0))
        pre = pre + dot(normed.astype(BF), weight(s, 1))
        pre = pre + dot(after(normed).astype(BF), weight(s, 2))
        sig = jax.nn.sigmoid(pre)
        slope[s] = sig * (1.0 + pre * (1.0 - sig))
        if s + 1 < SECTIONS:
            act = (pre * sig).astype(BF)
            result = x + dot(act, weight(s, 3))
            give_hidden(s + 1, result)
            hs[s + 1] = result.astype(BF)
        if s + 2 < SECTIONS:
            unless_own(s + 2, relay)
        if s == 2:
            each(YL, lambda i: y_copy(1, yl_of(i), yl_of(i)).wait_recv())
            ds[3] = s2d[1].reshape(ROWS, C)
            give_dense(3, ds[3].astype(F32))
    for s in (3, 2, 1):
        x, inv, normed = normalize(hs[s])
        grad = ds[s]
        dpre = dot_t(grad, weight(s, 3)) * slope[s]
        dnorm = dot_t(after(dpre).astype(BF), weight(s, 0))
        dnorm = dnorm + dot_t(dpre.astype(BF), weight(s, 1))
        dnorm = dnorm + dot_t(before(dpre).astype(BF), weight(s, 2))
        mean = jnp.mean(dnorm * normed, -1, keepdims=True)
        result = grad.astype(F32) + inv * (dnorm - normed * mean)
        give_dense(s - 1, result)
        if s > 1:
            ds[s - 1] = result.astype(BF)

    def micro(i):
        return x_of(i + jnp.where(i == 2, 1, 0) - jnp.where(i == 3, 1, 0))

    def taken(kept, value, send, recv, i):
        m = micro(i)

        @pl.when(i > 0)
        def _():
            remote(value.at[0], kept.at[m], send.at[0], recv.at[m], at_x(m)).wait_recv()

        return m

    def redo(i, _):
        m = taken(hr, packed_h, h_send, h_recv, i)
        low = hr[m, 2 * ROWS : WIDE].astype(F32)
        low = jnp.concatenate([low[:, 0:64], low[:, 64:128]], 0)
        wide = [hr[m, 0:ROWS].astype(F32), hr[m, ROWS : 2 * ROWS].astype(F32), low]
        x, inv, normed = normalize(jnp.concatenate(wide, 1))
        low = normed.astype(BF)
        pre = emb[pl.ds(m, 1), :] + dot(before(normed).astype(BF), weight(p, 0))
        pre = pre + dot(low, weight(p, 1))
        pre = pre + dot(after(normed).astype(BF), weight(p, 2))
        sig = jax.nn.sigmoid(pre)
        slope[m] = sig * (1.0 + pre * (1.0 - sig))
        lhs[0, m] = low
        lhs[1, m] = (pre * sig).astype(BF)
        return 0

    lax.fori_loop(0, SECTIONS, redo, 0)

    def redo_back(i, _):
        m = taken(dr, dense, d_send, d_recv, i)
        low = dr[m, 2 * ROWS : WIDE].astype(F32)
        low = jnp.concatenate([low[:, 0:64], low[:, 64:128]], 0).astype(BF)
        rhs[3, m, :, 0:128] = dr[m, 0:ROWS]
        rhs[3, m, :, 128:256] = dr[m, ROWS : 2 * ROWS]
        rhs[3, m, :, 256:320] = low
        dpre = dot_t(rhs[3, m], weight(p, 3)) * slope[m]
        rhs[0, m] = after(dpre).astype(BF)
        rhs[1, m] = dpre.astype(BF)
        rhs[2, m] = before(dpre).astype(BF)
        return 0

    lax.fori_loop(0, SECTIONS, redo_back, 0)

    def gradients(core, ref, then):
        tails = []
        for j in range(2):
            k = 2 * core + j
            term = t_dot(
                lhs[lax.div(k, 3)].reshape(SECTIONS * ROWS, C), rhs[k].reshape(SECTIONS * ROWS, C)
            )
            ref[2 * j * C : (2 * j + 1) * C, :] = term[:, 0:128].astype(ref.dtype)
            ref[(2 * j + 1) * C : (2 * j + 2) * C, :] = term[:, 128:256].astype(ref.dtype)
            tails.append(term[:, 256:320])
            if j:
                ref[4 * C : 5 * C, :] = jnp.concatenate(tails, 1).astype(ref.dtype)
                ref[5 * C : HALF, :] = jnp.zeros((HALF - 5 * C, 128), ref.dtype)
            then(j)

    def swap(j):
        part = pl.ds(2 * C * j, HALF - 2 * C if j else 2 * C)
        return remote(sb.at[part], rb.at[part], core_sem.at[0, j], core_sem.at[1, j], sibling)

    gradients(other, sb, lambda j: swap(j).start())
    gradients(c, gown, lambda j: None)
    for j, (lo, hi) in enumerate(((0, 2 * C), (2 * C, HALF))):
        swap(j).wait_recv()
        chip[lo:hi] = (gown[lo:hi] + rb[lo:hi].astype(F32)).astype(BF)

    def rows(start, size):
        return pl.ds(pl.multiple_of(start, 16), size)

    def a1(q, to, slot):
        lo, n = CHUNK_A[q]
        return remote(
            chip.at[rows(to * PA + lo, n)], ra.at[slot, pl.ds(lo, n)], a1s.at[q, to], a1r.at[q, slot], at_y(to)
        )

    def b1(q, to, slot):
        lo, n = CHUNK_B[q]
        return remote(
            chip.at[rows(HA + to * PB + lo, n)], rbz.at[slot, pl.ds(lo, n)], b1s.at[q, to], b1r.at[q, slot], at_z(to)
        )

    def a2(q, to, slot):
        ref = ra2.at[slot, pl.ds(*CHUNK_A[q])]
        return remote(ref, ref, a2s.at[q, to], a2r.at[q, slot], at_z(to))

    def b2(q, to, slot):
        ref = rb2.at[slot, pl.ds(*CHUNK_B[q])]
        return remote(ref, ref, b2s.at[q, to], b2r.at[q, slot], at_y(to))

    def a3(q, to, slot):
        lo, n = CHUNK_A[q]
        ref = fin.at[c, rows(slot * PA + lo, n)]
        return remote(ref, ref, a3s.at[q, to], a3r.at[q, slot], at_y(to))

    def b3(q, to, slot):
        lo, n = CHUNK_B[q]
        ref = fin.at[c, rows(HA + slot * PB + lo, n)]
        return remote(ref, ref, b3s.at[q, to], b3r.at[q, slot], at_z(to))

    def total(ref, chunk):
        lo, n = chunk
        value = ref[0, lo : lo + n].astype(F32)
        for i in range(1, 8):
            value = value + ref[i, lo : lo + n].astype(F32)
        return value.astype(BF)

    for q in range(CHUNKS):

        def first(i):
            a1(q, y_of(i), y).start()
            b1(q, z_of(i), z).start()

        far_first(first)
    ra[y] = chip[rows(y * PA, PA), :]
    rbz[z] = chip[rows(HA + z * PB, PB), :]
    for q in range(CHUNKS):
        lo, n = CHUNK_A[q]
        each(Y, lambda i: a1(q, y_of(i), y_of(i)).wait_recv())
        ra2[z, lo : lo + n] = total(ra, (lo, n))
        far_first(lambda i: a2(q, z_of(i), z).start())
        lo, n = CHUNK_B[q]
        each(Z, lambda i: b1(q, z_of(i), z_of(i)).wait_recv())
        rb2[y, lo : lo + n] = total(rbz, (lo, n))
        far_first(lambda i: b2(q, y_of(i), y).start())
    for q in range(CHUNKS):
        lo, n = CHUNK_A[q]
        each(Z, lambda i: a2(q, z_of(i), z_of(i)).wait_recv())
        fin[c, rows(y * PA + lo, n), :] = total(ra2, (lo, n))
        far_first(lambda i: a3(q, y_of(i), y).start())
        lo, n = CHUNK_B[q]
        each(Y, lambda i: b2(q, y_of(i), y_of(i)).wait_recv())
        fin[c, rows(HA + z * PB + lo, n), :] = total(rb2, (lo, n))
        far_first(lambda i: b3(q, z_of(i), z).start())

    def end(core, which):
        ref = fin.at[core, pl.ds(HA * which, HB if which else HA)]
        return remote(ref, ref, end_sem.at[0, which], end_sem.at[1, which], sibling)

    def store(core, which):
        part = pl.ds(HA * which, HB if which else HA)
        return pltpu.make_async_copy(fin.at[core, part], packed.at[core, part], out_sem.at[core, which])

    for q in range(CHUNKS):
        each(Y, lambda i: a3(q, y_of(i), y_of(i)).wait_recv())
    end(c, 0).start()
    store(c, 0).start()
    for q in range(CHUNKS):
        each(Z, lambda i: b3(q, z_of(i), z_of(i)).wait_recv())
    end(c, 1).start()
    store(c, 1).start()
    end(other, 0).wait_recv()
    store(other, 0).start()
    end(other, 1).wait_recv()
    store(other, 1).start()

    for to in (right, left, far):
        over_x(p, to).wait_send()
    for section in (left, right, far):
        for way in range(4):
            to_next(section, way, color).wait_send()
        for part in range(4):
            to_core(section, c, part).wait_send()
    for kind in range(2):
        each(Z, lambda i: z_copy(kind, z_of(i), z).wait_send())
        each(YL, lambda i: y_copy(kind, yl_of(i), yl).wait_send())

    def left_us(i):
        s = x_of(i)
        remote(packed_h.at[s], hr.at[p], h_send.at[s], h_recv.at[p], at_x(s)).wait_send()
        remote(dense.at[s], dr.at[p], d_send.at[s], d_recv.at[p], at_x(s)).wait_send()

    each(SECTIONS, left_us)
    swap(0).wait_send()
    swap(1).wait_send()
    for q in range(CHUNKS):

        def drained(i):
            a1(q, y_of(i), y).wait_send()
            b1(q, z_of(i), z).wait_send()
            a2(q, z_of(i), z).wait_send()
            b2(q, y_of(i), y).wait_send()
            a3(q, y_of(i), y).wait_send()
            b3(q, z_of(i), z).wait_send()

        each(Y, drained)
    for which in range(2):
        end(c, which).wait_send()
        store(c, which).wait()
        store(other, which).wait()


def unpack_kernel(scale, packed, conv_out, out_out, fin, full, in_sem, out_sem):
    loads = [pltpu.make_async_copy(packed.at[core], fin.at[core], in_sem.at[core]) for core in range(2)]
    for load in loads:
        load.start()
    stores = []
    for k in range(4):
        core, j = divmod(k, 2)
        if j == 0:
            loads[core].wait()
        full[k, :, 0:128] = fin[core, 2 * j * C : (2 * j + 1) * C, :].astype(F32) * scale
        full[k, :, 128:256] = fin[core, (2 * j + 1) * C : (2 * j + 2) * C, :].astype(F32) * scale
        tail = fin[core, 4 * C : 5 * C, :].astype(F32) * scale
        full[k, :, 256:320] = tail[:, 64 * j : 64 * j + 64]
        to = conv_out.at[0, k] if k < 3 else out_out.at[0]
        stores.append(pltpu.make_async_copy(full.at[k], to, out_sem.at[k]))
        stores[k].start()
    for store in stores:
        store.wait()


def body(video, cotangent, timesteps, conv_weight, out_weight):
    far_memory = pl.BlockSpec(memory_space=pltpu.HBM)
    dma = pltpu.SemaphoreType.DMA
    stack = (SECTIONS, ROWS, C)
    rows = video.shape[0] * 4 * 64 * video.shape[3]
    packed = pl.pallas_call(
        kernel,
        out_shape=jax.ShapeDtypeStruct((2, HALF, 128), BF),
        in_specs=[far_memory] * 5,
        out_specs=far_memory,
        scratch_shapes=[
            pltpu.VMEM((2, 64, C), BF),
            pltpu.VMEM((2, 64, C), BF),
            pltpu.VMEM((1, SECTIONS), jnp.int32),
            pltpu.VMEM((SECTIONS, C), F32),
            pltpu.VMEM((SECTIONS, 8, QUARTER, C), BF),
            pltpu.VMEM((2, Z, 16, C), BF),
            pltpu.VMEM((2, Z, 16, C), BF),
            pltpu.VMEM((2, YL, 32, C), BF),
            pltpu.VMEM((2, YL, 32, C), BF),
            pltpu.VMEM(stack, BF),
            pltpu.VMEM(stack, BF),
            pltpu.VMEM(stack, F32),
            pltpu.VMEM((SECTIONS, WIDE, 128), BF),
            pltpu.VMEM((SECTIONS, WIDE, 128), BF),
            pltpu.VMEM((SECTIONS, WIDE, 128), BF),
            pltpu.VMEM((SECTIONS, WIDE, 128), BF),
            pltpu.VMEM((2, *stack), BF),
            pltpu.VMEM((4, *stack), BF),
            pltpu.VMEM((HALF, 128), F32),
            pltpu.VMEM((HALF, 128), BF),
            pltpu.VMEM((HALF, 128), BF),
            pltpu.VMEM((HALF, 128), BF),
            pltpu.VMEM((8, PA, 128), BF),
            pltpu.VMEM((8, PB, 128), BF),
            pltpu.VMEM((8, PA, 128), BF),
            pltpu.VMEM((8, PB, 128), BF),
            pltpu.VMEM((2, HALF, 128), BF),
            dma((5,)),
            dma((2, Z)), dma((2, Z)), dma((2, YL)), dma((2, YL)),
            dma((SECTIONS,)), dma((SECTIONS,)),
            dma((SECTIONS, 4)), dma((SECTIONS, 4)), dma((SECTIONS, 4)), dma((SECTIONS, 4)),
            dma((SECTIONS,)), dma((SECTIONS,)), dma((SECTIONS,)), dma((SECTIONS,)),
            dma((2, 2)),
        ]
        + [dma((CHUNKS, 8))] * 12
        + [dma((2, 2))] * 2,
        compiler_params=pltpu.CompilerParams(
            collective_id=1, has_side_effects=True, vmem_limit_bytes=56 << 20
        ),
        name="main",
    )(
        video,
        cotangent,
        timesteps.T,
        conv_weight.reshape(1, 6, QUARTER, C),
        out_weight.reshape(1, 2, QUARTER, C),
    )
    return pl.pallas_call(
        functools.partial(unpack_kernel, 1.0 / math.sqrt(rows)),
        out_shape=(
            jax.ShapeDtypeStruct((1, 3, C, C), F32),
            jax.ShapeDtypeStruct((1, C, C), F32),
        ),
        in_specs=[far_memory],
        out_specs=(far_memory, far_memory),
        scratch_shapes=[
            pltpu.VMEM((2, HALF, 128), BF),
            pltpu.VMEM((4, C, C), F32),
            dma((2,)),
            dma((4,)),
        ],
        compiler_params=pltpu.CompilerParams(vmem_limit_bytes=56 << 20),
        name="unpack",
    )(packed)


def solution(mesh):
    return jax.shard_map(
        body,
        mesh=mesh,
        in_specs=(
            P(None, "dp", "tm", None, None),
            P(None, "dp", "tm", None, None),
            P(None, "dp"),
            P("pipe", None, None, None),
            P("pipe", None, None),
        ),
        out_specs=(P("pipe", None, None, None), P("pipe", None, None)),
        check_vma=False,
    )
```
